256 devices in a mesh: dp: 32 (over z, y), tensor: 8 (over x, core).
Axes of the slice: x: 4, y: 4, z: 8, core: 2. Of those that a mesh axis runs over, the one named last changes fastest.
Arguments:
- x_in: bfloat16 [8192, 16384], P('dp', 'tensor'), may hold values from -125 to 125, as said below
- grad_up: bfloat16 [8192, 53248], P('dp', 'tensor'), may hold values from -125 to 125, as said below
- hidden_act: bfloat16 [8192, 53248], P('dp', 'tensor'), may hold values from -125 to 125, as said below
- grad_down: bfloat16 [8192, 16384], P('dp', 'tensor'), may hold values from -125 to 125, as said below
- sketch_up: bfloat16 [32, 53248], P(None, 'tensor'), may hold values from -4 to 4
- sketch_down: bfloat16 [32, 16384], P(None, 'tensor'), may hold values from -4 to 4
Outputs:
- up_a: float32 [32, 16384], P(None, 'tensor')
- up_b: float32 [32, 53248], P(None, 'tensor')
- down_a: float32 [32, 53248], P(None, 'tensor')
- down_b: float32 [32, 16384], P(None, 'tensor')
The draws below stay inside these ranges and needn't reach their ends.
Inputs may be any that keep to these rules, and one draw needn't show every extreme that they name: `x_in`: Real-valued entries of order one to some tens; row and column scales vary. `grad_up`: Real-valued entries of order one to some tens; row and column scales vary. `hidden_act`: Real-valued entries of order one to some tens; row and column scales vary. `grad_down`: Real-valued entries of order one to some tens; row and column scales vary.
All inputs are finite; a program needn't handle non-finite values.
Results may differ from the reference program's by a relative error of at most 0.014.
Values may be sent and summed in bfloat16 or wider, within the bound.
A program may use at most 64 MiB of HBM per device.

```python
import math
import jax
import jax.numpy as jnp
from jax import lax

D = 16384
FF = 53248
R = 32
ITERS = 2
TOKENS = 8192


low_terms = 48


low_decay = 0.93


low_ratio = 10.0


def scale_profile(key, rows, cols, rise):
    row_key, col_key = jax.random.split(key)
    row_pos = jnp.arange(rows, dtype=jnp.float32) / rows - 0.5
    col_pos = jnp.arange(cols, dtype=jnp.float32) / cols - 0.5
    row_scale = jnp.power(rise, row_pos) * jnp.exp(jax.random.uniform(row_key, (rows,), jnp.float32, -0.6, 0.6))
    col_scale = jnp.power(rise, col_pos) * jnp.exp(jax.random.uniform(col_key, (cols,), jnp.float32, -0.6, 0.6))
    return row_scale[:, None] * col_scale[None, :]


def normal_field(key, rows, cols):
    return jax.random.normal(key, (rows, cols), jnp.float32)


def token_factor(key, salt):
    return jax.random.normal(jax.random.fold_in(key, salt), (TOKENS, low_terms), jnp.float32)


def low_part(token_part, key, cols):
    strength = math.sqrt(low_ratio * (math.sqrt(D) + math.sqrt(FF)) / math.sqrt(float(TOKENS) * float(D) * float(FF)))
    weights = strength * jnp.power(low_decay, jnp.arange(low_terms, dtype=jnp.float32))
    feature = jax.random.normal(key, (cols, low_terms), jnp.float32)
    return jnp.dot(token_part * weights[None, :], feature.T, precision=lax.Precision.HIGHEST, preferred_element_type=jnp.float32)


def combine_field(noise, lowrank, profile):
    return (jnp.clip(noise + lowrank, -4.0, 4.0) * profile).astype(jnp.bfloat16)


def draw_x_in(key, part):
    token_part = token_factor(key, 101)
    key = jax.random.fold_in(key, 11)
    base_key, scale_key, low_key = jax.random.split(key, 3)
    lowrank = low_part(token_part, low_key, D)
    return combine_field(normal_field(base_key, TOKENS, D), lowrank, scale_profile(scale_key, TOKENS, D, 3.0))


def draw_grad_up(key, part):
    token_part = token_factor(key, 101)
    key = jax.random.fold_in(key, 23)
    base_key, scale_key, low_key = jax.random.split(key, 3)
    lowrank = low_part(token_part, low_key, FF)
    return combine_field(normal_field(base_key, TOKENS, FF), lowrank, scale_profile(scale_key, TOKENS, FF, 3.0))


def draw_hidden_act(key, part):
    token_part = token_factor(key, 202)
    key = jax.random.fold_in(key, 37)
    base_key, scale_key, low_key = jax.random.split(key, 3)
    lowrank = low_part(token_part, low_key, FF)
    return combine_field(normal_field(base_key, TOKENS, FF), lowrank, scale_profile(scale_key, TOKENS, FF, 3.0))


def draw_grad_down(key, part):
    token_part = token_factor(key, 202)
    key = jax.random.fold_in(key, 41)
    base_key, scale_key, low_key = jax.random.split(key, 3)
    lowrank = low_part(token_part, low_key, D)
    return combine_field(normal_field(base_key, TOKENS, D), lowrank, scale_profile(scale_key, TOKENS, D, 3.0))


def levels(own_key, shape, cuts, smallest, largest):
    loudness = 1.0
    for dim, shards_of in cuts:
        heights = jax.random.uniform(jax.random.fold_in(jax.random.fold_in(own_key, 6), dim), (shards_of,), jnp.float32, smallest / len(cuts), largest / len(cuts))
        loudness = loudness * jnp.repeat(jnp.exp(heights), shape[dim] // shards_of).reshape((-1,) + (1,) * (len(shape) - 1 - dim))
    return loudness


def centred(own_key, extent, deviation, bound, cuts=(), kind=jnp.bfloat16):
    level = levels(own_key, extent, cuts, -0.22, 0.18) if cuts else 1.0
    values = jax.random.normal(own_key, extent, jnp.float32) * deviation * level
    return jnp.minimum(jnp.maximum(values, -bound), bound).astype(kind)


def setup_inputs(seed: int = 0) -> dict:
    keys = jax.random.split(jax.random.key(seed), 7)
    x_in = draw_x_in(jax.random.fold_in(keys[6], 71), 0)
    grad_up = draw_grad_up(jax.random.fold_in(keys[6], 71), 0)
    hidden_act = draw_hidden_act(jax.random.fold_in(keys[6], 71), 0)
    grad_down = draw_grad_down(jax.random.fold_in(keys[6], 71), 0)
    sketch_up = centred(keys[4], (R, FF), 1.0, 4.0, ((1, 8),))
    sketch_down = centred(keys[5], (R, D), 1.0, 4.0, ((1, 8),))
    return dict(x_in=x_in, grad_up=grad_up, hidden_act=hidden_act, grad_down=grad_down, sketch_up=sketch_up, sketch_down=sketch_down)


def orthonormal(panel):
    gram = jnp.dot(panel.astype(jnp.float32), panel.T.astype(jnp.float32), precision=lax.Precision.HIGHEST, preferred_element_type=jnp.float32)
    lower = jnp.linalg.cholesky(gram)
    return jax.scipy.linalg.solve_triangular(lower, panel, lower=True).astype(jnp.bfloat16)

def apply_pair(left, right, panel):
    token_side = jnp.dot(panel.astype(jnp.float32), right.T.astype(jnp.float32), preferred_element_type=jnp.float32).astype(jnp.bfloat16)
    return jnp.dot(token_side.astype(jnp.float32), left.astype(jnp.float32), preferred_element_type=jnp.float32)

def reference(x_in, grad_up, hidden_act, grad_down, sketch_up, sketch_down):
    up_q = orthonormal(apply_pair(x_in, grad_up, sketch_up))
    down_q = orthonormal(apply_pair(hidden_act, grad_down, sketch_down))
    for step in range(ITERS):
        up_p = orthonormal(apply_pair(grad_up, x_in, up_q))
        down_p = orthonormal(apply_pair(grad_down, hidden_act, down_q))
        up_q = orthonormal(apply_pair(x_in, grad_up, up_p))
        down_q = orthonormal(apply_pair(hidden_act, grad_down, down_p))
    scale = 1.0 / math.sqrt(TOKENS)
    up_a = up_q.astype(jnp.float32) * math.sqrt(D)
    down_a = down_q.astype(jnp.float32) * math.sqrt(FF)
    up_b = apply_pair(grad_up, x_in, up_q) * scale
    down_b = apply_pair(grad_down, hidden_act, down_q) * scale
    return (up_a, up_b, down_a, down_b)
```

```python
import functools
import math

import jax
import jax.numpy as jnp
from jax import lax
from jax.experimental import pallas as pl
from jax.experimental.pallas import tpu as pltpu
from jax.sharding import PartitionSpec as P

MESH = pl.DeviceIdType.MESH

NZ, NY, NX, NC = 8, 4, 4, 2
R = 32
ITERS = 2
ROUNDS = 2 * ITERS + 2
HALF = R // 2
LANES = 128
GROUPS = NZ // 2
SLOTS = NZ * NY

FAR = (4, 3, 5, 2, 6, 1, 7)
NEAR = (1, 7, 2, 6, 3, 5, 4)


def nt_dot(a, b):
    return lax.dot_general(a, b, (((1,), (1,)), ((), ())), preferred_element_type=jnp.float32)


def nn_dot(a, b, precision=None):
    return lax.dot_general(
        a, b, (((1,), (0,)), ((), ())), precision=precision, preferred_element_type=jnp.float32
    )


def invert_factor(gram):
    lane = lax.broadcasted_iota(jnp.int32, (R, LANES), 1)
    row = lax.broadcasted_iota(jnp.int32, (R, LANES), 0)
    wide = lane < 64
    right = (lane % 64) >= R
    eye = jnp.where((lane % 64) - R == row, 1.0, 0.0)
    work = jnp.where(right, eye, gram)
    pivots = jnp.zeros((R, LANES), jnp.float32)
    for k in range(R):
        column = jnp.where(
            wide,
            jnp.broadcast_to(work[:, k : k + 1], (R, LANES)),
            jnp.broadcast_to(work[:, 64 + k : 65 + k], (R, LANES)),
        )
        pivot = jnp.broadcast_to(column[k : k + 1, :], (R, LANES))
        pivots = jnp.where(row == k, pivot, pivots)
        factor = jnp.where(row > k, column / pivot, 0.0)
        work = work - factor * jnp.broadcast_to(work[k : k + 1, :], (R, LANES))
    return jnp.where(right, work * lax.rsqrt(pivots), 0.0)


def kernel(
    x_in, grad_up, hidden_act, grad_down, sketch_up, sketch_down,
    up_a, up_b, down_a, down_b,
    wide, narrow, sk_wide, sk_narrow, panel, ysend, yrecv, zown, zsend, zrecv,
    us, uc, ux, kparts, kbuf,
    in_sem, ys_sem, yr_sem, zs_sem, zr_sem, ag_sem, agz_sem, agy_sem,
    ks_sem, kr_sem, ucs_sem, ucr_sem, uxs_sem, uxr_sem,
):
    dp = lax.axis_index("dp")
    me_t = lax.axis_index("tensor")
    z, y = dp // NY, dp % NY
    x, c = me_t // NC, me_t % NC
    slot = dp
    tiles_wide = wide.shape[2] // LANES // GROUPS
    tiles_narrow = narrow.shape[2] // LANES // GROUPS
    span = tiles_wide // NY
    cols_wide = tiles_wide * LANES
    cols_narrow = tiles_narrow * LANES
    tokens = wide.shape[1]

    loads = [
        pltpu.make_async_copy(src, dst, in_sem.at[i])
        for i, (src, dst) in enumerate(
            (
                (sketch_up, sk_wide),
                (sketch_down, sk_narrow),
                (grad_up, wide.at[0]),
                (grad_down, narrow.at[1]),
                (x_in, narrow.at[0]),
                (hidden_act, wide.at[1]),
            )
        )
    ]
    for load in loads:
        load.start()

    def dev_zy(zz, yy):
        return (zz * NY + yy, me_t)

    def dev_t(tt):
        return (dp, tt)

    barrier = pltpu.get_barrier_semaphore()
    peers = [dev_zy((z + o) % NZ, y) for o in range(1, NZ)]
    peers += [dev_zy(z, (y + o) % NY) for o in range(1, NY)]
    peers += [dev_t((me_t + o) % (NX * NC)) for o in range(1, NX * NC)]
    for peer in peers:
        pl.semaphore_signal(barrier, inc=1, device_id=peer, device_id_type=MESH)

    for load in loads:
        load.wait()

    for k in range(GROUPS):
        for h in range(2):
            for yy in range(NY):
                s = (2 * k + h) * NY + yy
                rows = slice(HALF * h, HALF * h + HALF)
                for i in range(span + 1):
                    lo = (k * tiles_wide + yy * span + i) * LANES
                    panel[0, s, i] = sk_wide[rows, lo : lo + LANES]
                lo = (k * tiles_narrow + yy) * LANES
                panel[0, s, span + 1] = sk_narrow[rows, lo : lo + LANES]

    pl.semaphore_wait(barrier, len(peers))

    def unpack(r, kk):
        wide_tiles, narrow_tiles = [], []
        for t in range(tiles_wide):
            yy = min(t // span, NY - 1)
            i = t - span * yy
            wide_tiles.append(
                jnp.concatenate([panel[r, (2 * kk + h) * NY + yy, i] for h in range(2)], axis=0)
            )
        for yy in range(NY):
            narrow_tiles.append(
                jnp.concatenate([panel[r, (2 * kk + h) * NY + yy, span + 1] for h in range(2)], axis=0)
            )
        return jnp.concatenate(wide_tiles, axis=1), jnp.concatenate(narrow_tiles, axis=1)

    def wait_gather(kk):
        part = panel.at[0, pl.ds(0, 2 * (NY - 1))]
        pltpu.make_async_copy(part, part, agy_sem.at[kk]).wait()

    def wait_sends():
        for buf, n, sem in (
            (ysend.at[0], NZ * (NY - 1), ys_sem),
            (zsend.at[0], NZ - 1, zs_sem),
            (panel.at[0], NZ - 1 + NZ * (NY - 1), ag_sem),
            (kbuf.at[0], NX * NC - 1, ks_sem),
            (us, 1, ucs_sem),
            (ux.at[0], (NX - 1) * NC, uxs_sem),
        ):
            part = buf.at[pl.ds(0, n)]
            pltpu.make_async_copy(part, part, sem).wait()

    def one_round(r, _):
        par = r % 2
        sum_wide = jnp.zeros((R, tokens), jnp.float32)
        sum_narrow = jnp.zeros((R, tokens), jnp.float32)
        for o in (0, 1, 3, 2):
            kk = (z // 2 + o) % GROUPS

            @pl.when(r > 0)
            def _():
                wait_gather(kk)

            pw, pn = unpack(r, kk)
            at_wide = pl.ds(pl.multiple_of(kk * cols_wide, LANES), cols_wide)
            at_narrow = pl.ds(pl.multiple_of(kk * cols_narrow, LANES), cols_narrow)
            kparts[kk, 0] = nt_dot(pw, pw)
            kparts[kk, 1] = nt_dot(pn, pn)
            sum_wide = sum_wide + nt_dot(pw, wide[par, :, at_wide])
            sum_narrow = sum_narrow + nt_dot(pn, narrow[1 - par, :, at_narrow])

        kw = ((kparts[0, 0] + kparts[1, 0]) + kparts[2, 0]) + kparts[3, 0]
        kn = ((kparts[0, 1] + kparts[1, 1]) + kparts[2, 1]) + kparts[3, 1]
        blank = jnp.zeros((R, R), jnp.float32)
        kbuf[r, me_t] = jnp.concatenate([kw, blank, kn, blank], axis=1)
        us[r, 0] = sum_wide
        us[r, 1] = sum_narrow
        pltpu.make_async_remote_copy(
            us.at[r], uc.at[r], ucs_sem, ucr_sem.at[r],
            device_id=dev_t(x * NC + 1 - c), device_id_type=MESH,
        ).start()
        for o in range(1, NX * NC):
            pltpu.make_async_remote_copy(
                kbuf.at[r, me_t], kbuf.at[r, me_t], ks_sem, kr_sem.at[r],
                device_id=dev_t((me_t + o) % (NX * NC)), device_id_type=MESH,
            ).start()

        pltpu.make_async_copy(us.at[r], uc.at[r], ucr_sem.at[r]).wait()
        ux[r, x * NC] = (us[r, 0] + uc[r, 0]).astype(jnp.bfloat16)
        ux[r, x * NC + 1] = (us[r, 1] + uc[r, 1]).astype(jnp.bfloat16)
        for o in range(1, NX):
            for cc in range(NC):
                pltpu.make_async_remote_copy(
                    ux.at[r, me_t], ux.at[r, me_t], uxs_sem, uxr_sem.at[r],
                    device_id=dev_t(((x + o) % NX) * NC + cc), device_id_type=MESH,
                ).start()

        part = kbuf.at[r, pl.ds(0, NX * NC - 1)]
        pltpu.make_async_copy(part, part, kr_sem.at[r]).wait()
        gram = kbuf[r, 0]
        for t in range(1, NX * NC):
            gram = gram + kbuf[r, t]
        lane = lax.broadcasted_iota(jnp.int32, (R, LANES), 1)
        row = lax.broadcasted_iota(jnp.int32, (R, LANES), 0)
        identity = jnp.where((lane % 64) - R == row, 1.0, 0.0)
        inverse = jnp.where(jnp.full((R, LANES), r) == 0, identity, invert_factor(gram))
        inv_wide = inverse[:, R : 2 * R]
        inv_narrow = inverse[:, 64 + R : 64 + 2 * R]

        part = ux.at[r, pl.ds(0, (NX - 1) * NC)]
        pltpu.make_async_copy(part, part, uxr_sem.at[r]).wait()
        tok = []
        for h, inv in enumerate((inv_wide, inv_narrow)):
            total = ux[r, h].astype(jnp.float32)
            for xx in range(1, NX):
                total = total + ux[r, xx * NC + h].astype(jnp.float32)
            tok.append(nn_dot(inv, total, lax.Precision.HIGHEST).astype(jnp.bfloat16))
        tok_wide, tok_narrow = tok

        for o in (2, 1, 3, 0):
            kk = (z // 2 + o) % GROUPS
            at_wide = pl.ds(pl.multiple_of(kk * cols_wide, LANES), cols_wide)
            at_narrow = pl.ds(pl.multiple_of(kk * cols_narrow, LANES), cols_narrow)
            pw = nn_dot(tok_narrow, wide[1 - par, :, at_wide]).astype(jnp.bfloat16)
            pn = nn_dot(tok_wide, narrow[par, :, at_narrow]).astype(jnp.bfloat16)
            for h in range(2):
                rows = slice(HALF * h, HALF * h + HALF)
                for yy in range(NY):
                    s = (2 * kk + h) * NY + yy
                    for i in range(span + 1):
                        lo = (yy * span + i) * LANES
                        ysend[r, s, i] = pw[rows, lo : lo + LANES]
                    ysend[r, s, span + 1] = pn[rows, yy * LANES : (yy + 1) * LANES]
            for h in range(2):
                zd = 2 * kk + h
                for q in range(1, NY):
                    yd = (y + q) % NY
                    pltpu.make_async_remote_copy(
                        ysend.at[r, zd * NY + yd], yrecv.at[r, zd, q - 1], ys_sem, yr_sem.at[zd],
                        device_id=dev_zy(z, yd), device_id_type=MESH,
                    ).start()

        @pl.when(r == ROUNDS - 1)
        def _():
            total_wide = wide.shape[2] * NX * NC
            total_narrow = narrow.shape[2] * NX * NC
            for k in range(GROUPS):
                pw, pn = unpack(r, k)
                for inv, pan, out, cols, total in (
                    (inv_wide, pw, down_a, cols_wide, total_wide),
                    (inv_narrow, pn, up_a, cols_narrow, total_narrow),
                ):
                    q = nn_dot(inv, pan.astype(jnp.float32), lax.Precision.HIGHEST)
                    q = q.astype(jnp.bfloat16).astype(jnp.float32) * math.sqrt(total)
                    out[:, k * cols : (k + 1) * cols] = q

        for o in FAR + (0,):
            zd = (z + o) % NZ
            part = yrecv.at[r, zd]
            pltpu.make_async_copy(part, part, yr_sem.at[zd]).wait()
            total = ysend[r, zd * NY + y].astype(jnp.float32)
            for q in range(NY - 1):
                total = total + yrecv[r, zd, q].astype(jnp.float32)
            if o:
                zsend[r, zd] = total.astype(jnp.bfloat16)
                pltpu.make_async_remote_copy(
                    zsend.at[r, zd], zrecv.at[r, o - 1], zs_sem, zr_sem,
                    device_id=dev_zy(zd, y), device_id_type=MESH,
                ).start()
            else:
                zown[...] = total
        part = zrecv.at[r]
        pltpu.make_async_copy(part, part, zr_sem).wait()
        total = zown[...]
        for q in range(NZ - 1):
            total = total + zrecv[r, q].astype(jnp.float32)
        panel[r + 1, slot] = total.astype(jnp.bfloat16)

        def to_y(zs):
            s = zs * NY + y
            for q in range(1, NY):
                pltpu.make_async_remote_copy(
                    panel.at[r + 1, s], panel.at[r + 1, s], ag_sem, agy_sem.at[zs // 2],
                    device_id=dev_zy(z, (y + q) % NY), device_id_type=MESH,
                ).start()

        for o in FAR:
            pltpu.make_async_remote_copy(
                panel.at[r + 1, slot], panel.at[r + 1, slot], ag_sem, agz_sem.at[o - 1],
                device_id=dev_zy((z + o) % NZ, y), device_id_type=MESH,
            ).start()
        to_y(z)
        for o in NEAR:
            zs = (z + NZ - o) % NZ
            part = panel.at[r + 1, zs * NY + y]
            pltpu.make_async_copy(part, part, agz_sem.at[o - 1]).wait()
            to_y(zs)
        wait_sends()
        return 0

    lax.fori_loop(0, ROUNDS, one_round, 0)

    scale = 1.0 / math.sqrt(tokens * NZ * NY)
    for k in range(GROUPS):
        wait_gather(k)
    for k in range(GROUPS):
        pw, pn = unpack(ROUNDS, k)
        up_b[:, k * cols_wide : (k + 1) * cols_wide] = pw.astype(jnp.float32) * scale
        down_b[:, k * cols_narrow : (k + 1) * cols_narrow] = pn.astype(jnp.float32) * scale


def local(x_in, grad_up, hidden_act, grad_down, sketch_up, sketch_down):
    tokens, n_narrow = x_in.shape
    n_wide = grad_up.shape[1]
    piece = (n_wide // LANES // GROUPS // NY + 2, HALF, LANES)
    bf16, f32 = jnp.bfloat16, jnp.float32
    dma = pltpu.SemaphoreType.DMA
    vmem = pltpu.VMEM
    scratch = [
        vmem((2, tokens, n_wide), bf16),
        vmem((2, tokens, n_narrow), bf16),
        vmem((R, n_wide), bf16),
        vmem((R, n_narrow), bf16),
        vmem((ROUNDS + 1, SLOTS) + piece, bf16),
        vmem((ROUNDS, SLOTS) + piece, bf16),
        vmem((ROUNDS, NZ, NY - 1) + piece, bf16),
        vmem(piece, f32),
        vmem((ROUNDS, NZ) + piece, bf16),
        vmem((ROUNDS, NZ - 1) + piece, bf16),
        vmem((ROUNDS, 2, R, tokens), f32),
        vmem((ROUNDS, 2, R, tokens), f32),
        vmem((ROUNDS, NX * NC, R, tokens), bf16),
        vmem((GROUPS, 2, R, R), f32),
        vmem((ROUNDS, NX * NC, R, LANES), f32),
        dma((6,)), dma, dma((NZ,)), dma, dma, dma, dma((NZ - 1,)), dma((GROUPS,)),
        dma, dma((ROUNDS,)), dma, dma((ROUNDS,)), dma, dma((ROUNDS,)),
    ]
    out_shape = (
        jax.ShapeDtypeStruct((R, n_narrow), f32),
        jax.ShapeDtypeStruct((R, n_wide), f32),
        jax.ShapeDtypeStruct((R, n_wide), f32),
        jax.ShapeDtypeStruct((R, n_narrow), f32),
    )
    return pl.pallas_call(
        kernel,
        out_shape=out_shape,
        in_specs=[pl.BlockSpec(memory_space=pl.ANY)] * 6,
        out_specs=[pl.BlockSpec(memory_space=pltpu.VMEM)] * 4,
        scratch_shapes=scratch,
        compiler_params=pltpu.CompilerParams(
            collective_id=0, has_side_effects=True, vmem_limit_bytes=56 * 2**20
        ),
    )(x_in, grad_up, hidden_act, grad_down, sketch_up, sketch_down)


def solution(mesh):
    in_specs = (
        P("dp", "tensor"),
        P("dp", "tensor"),
        P("dp", "tensor"),
        P("dp", "tensor"),
        P(None, "tensor"),
        P(None, "tensor"),
    )
    out_specs = (P(None, "tensor"), P(None, "tensor"), P(None, "tensor"), P(None, "tensor"))
    return jax.shard_map(local, mesh=mesh, in_specs=in_specs, out_specs=out_specs, check_vma=False)
```

```python
import functools
import math

import jax
import jax.numpy as jnp
from jax import lax
from jax.experimental import pallas as pl
from jax.experimental.pallas import tpu as pltpu
from jax.sharding import PartitionSpec as P

MESH = pl.DeviceIdType.MESH

NZ, NY, NX, NC = 8, 4, 4, 2
R = 32
ITERS = 2
PAIRS = ITERS + 1
HALF = R // 2
LANES = 128
GROUPS = NZ // 2
SLOTS = NZ * NY
NT = NX * NC
BLOCK = 16

FAR = (4, 3, 5, 2, 6, 1, 7)
NEAR = (1, 7, 2, 6, 3, 5, 4)


def nt_dot(a, b):
    return lax.dot_general(a, b, (((1,), (1,)), ((), ())), preferred_element_type=jnp.float32)


def nn_dot(a, b, precision=None):
    return lax.dot_general(
        a, b, (((1,), (0,)), ((), ())), precision=precision, preferred_element_type=jnp.float32
    )


def invert_factor(gram):
    lane = lax.broadcasted_iota(jnp.int32, (R, LANES), 1)
    row = lax.broadcasted_iota(jnp.int32, (R, LANES), 0)
    right = lane >= R
    padded = jnp.concatenate([gram, jnp.zeros((R, LANES - R), jnp.float32)], axis=1)
    work = jnp.where(right, jnp.where(lane - R == row, 1.0, 0.0), padded)
    scale = jnp.zeros((R, LANES), jnp.float32)
    for b in range(0, R, BLOCK):
        cols = [jnp.broadcast_to(work[:, b + j : b + j + 1], (R, LANES)) for j in range(BLOCK)]
        for j in range(BLOCK):
            k = b + j
            pivot = jnp.broadcast_to(cols[j][k : k + 1, :], (R, LANES))
            scale = jnp.where(row == k, lax.rsqrt(pivot), scale)
            factor = jnp.where(row > k, cols[j] * (1.0 / pivot), 0.0)
            for i in range(j + 1, BLOCK):
                cols[i] = cols[i] - factor * jnp.broadcast_to(cols[i][k : k + 1, :], (R, LANES))
            work = work - factor * jnp.broadcast_to(work[k : k + 1, :], (R, LANES))
    return (work * scale)[:, R : 2 * R]


def settle(ref, sem):
    pltpu.make_async_copy(ref, ref, sem).wait()


def kernel(
    x_in, grad_up, hidden_act, grad_down, sketch_up, sketch_down,
    up_q, up_img, down_q, down_img,
    x_v, gu_v, h_v, gd_v, sk_wide, sk_narrow, qn_v, qw_v,
    up_wide, up_narrow, dn_wide, dn_narrow,
    ysend, yrecv, zown, zsend, zrecv, nsend, nrecv,
    us, uc, ux, kparts, kbuf,
    in_sem, out_sem, ys_sem, yr_sem, zs_sem, zr_sem, ag_sem, agz_sem, agy_sem,
    ns_sem, nr_sem, nag_sem, nagr_sem, ks_sem, kr_sem, ucs_sem, ucr_sem, uxs_sem, uxr_sem,
):
    dp = lax.axis_index("dp")
    me_t = lax.axis_index("tensor")
    z, y = dp // NY, dp % NY
    x, c = me_t // NC, me_t % NC
    slot = dp
    n_wide, n_narrow = gu_v.shape[1], x_v.shape[1]
    tiles = n_wide // LANES // GROUPS
    span = tiles // NY
    cols = tiles * LANES
    tokens = gu_v.shape[0]

    loads = [
        pltpu.make_async_copy(src, dst, in_sem.at[i])
        for i, (src, dst) in enumerate(
            (
                (sketch_down, sk_narrow),
                (sketch_up, sk_wide),
                (grad_down, gd_v),
                (grad_up, gu_v),
                (hidden_act, h_v),
                (x_in, x_v),
            )
        )
    ]
    for load in loads:
        load.start()

    def dev_dp(zz, yy):
        return (zz * NY + yy, me_t)

    def dev_t(tt):
        return (dp, tt)

    def send(src, dst, send_sem, recv_sem, device):
        pltpu.make_async_remote_copy(
            src, dst, send_sem, recv_sem, device_id=device, device_id_type=MESH
        ).start()

    barrier = pltpu.get_barrier_semaphore()
    peers = [((dp + o) % SLOTS, me_t) for o in range(1, SLOTS)]
    peers += [dev_t((me_t + o) % NT) for o in range(1, NT)]
    for peer in peers:
        pl.semaphore_signal(barrier, inc=1, device_id=peer, device_id_type=MESH)

    for load in loads[:4]:
        load.wait()

    for k in range(GROUPS):
        for h in range(2):
            rows = slice(HALF * h, HALF * h + HALF)
            for yy in range(NY):
                s = (2 * k + h) * NY + yy
                for i in range(span + 1):
                    lo = (k * tiles + yy * span + i) * LANES
                    up_wide[0, s, i] = sk_wide[rows, lo : lo + LANES]
                lo = (k * NY + yy) * LANES
                dn_narrow[0, s] = sk_narrow[rows, lo : lo + LANES]

    pl.semaphore_wait(barrier, len(peers))

    def wide_group(panel, i, kk):
        out = []
        for t in range(tiles):
            yy = min(t // span, NY - 1)
            out.append(
                jnp.concatenate(
                    [panel[i, (2 * kk + h) * NY + yy, t - span * yy] for h in range(2)], axis=0
                )
            )
        return jnp.concatenate(out, axis=1)

    def narrow_all(panel, i):
        out = []
        for t in range(SLOTS // 2):
            k, yy = t // NY, t % NY
            out.append(
                jnp.concatenate([panel[i, (2 * k + h) * NY + yy] for h in range(2)], axis=0)
            )
        return jnp.concatenate(out, axis=1)

    def send_gram(cp, d, gram):
        packed = jnp.concatenate([gram[8 * j : 8 * j + 8, :] for j in range(R // 8)], axis=1)
        kbuf[cp, d, me_t] = packed
        mine = kbuf.at[cp, d, me_t]
        for o in (1, 2, 3, 4, 5, 6, 7):
            send(mine, mine, ks_sem.at[cp], kr_sem.at[cp, d], dev_t((me_t + o) % NT))

    def send_core(cp, d, total):
        us[cp, d] = total
        send(us.at[cp, d], uc.at[cp, d], ucs_sem.at[cp], ucr_sem.at[cp, d], dev_t(x * NC + 1 - c))

    def past_sends(cp, d):
        @pl.when(d > 0)
        def _():
            last_tensor(cp)

    def last_tensor(cp):
        settle(kbuf.at[cp, 0, pl.ds(0, NT - 1)], ks_sem.at[cp])
        settle(us.at[cp, 0], ucs_sem.at[cp])
        settle(ux.at[cp, 0, pl.ds(0, (NX - 1) * NC)], uxs_sem.at[cp])

    def last_wide(w):
        settle(ysend.at[w, 0, pl.ds(0, NZ * (NY - 1))], ys_sem.at[w])
        settle(zsend.at[w, 0, pl.ds(0, NZ - 1)], zs_sem.at[w])
        settle(up_wide.at[0, pl.ds(0, SLOTS - 1)], ag_sem.at[w])

    def last_narrow(w):
        settle(nsend.at[w, 0, pl.ds(0, SLOTS - 1)], ns_sem.at[w])
        settle(up_narrow.at[0, pl.ds(0, SLOTS - 1)], nag_sem.at[w])

    def wait_wide(w, kk):
        settle(up_wide.at[0, pl.ds(0, 2 * (NY - 1))], agy_sem.at[w, kk])

    def wait_narrow(w):
        settle(up_narrow.at[0, pl.ds(0, SLOTS - 1)], nagr_sem.at[w])

    def sums_wide(cp, d, panel, w, rows, fresh):
        past_sends(cp, d)
        total = jnp.zeros((R, tokens), jnp.float32)
        for n, o in enumerate((0, 1, 3, 2)):
            kk = (z // 2 + o) % GROUPS
            if fresh:
                wait_wide(w, kk)
            else:

                @pl.when(d > 0)
                def _():
                    wait_wide(w, kk)

            part = wide_group(panel, d, kk)
            kparts[kk] = nt_dot(part, part)
            if n == GROUPS - 1:
                send_gram(cp, d, ((kparts[0] + kparts[1]) + kparts[2]) + kparts[3])
            at = pl.ds(pl.multiple_of(kk * cols, LANES), cols)
            total = total + nt_dot(part, rows[:, at])
        send_core(cp, d, total)

    def sums_narrow(cp, d, panel, w, rows, fresh):
        past_sends(cp, d)
        if fresh:
            wait_narrow(w)
        else:

            @pl.when(d > 0)
            def _():
                wait_narrow(w)

        part = narrow_all(panel, d)
        send_gram(cp, d, nt_dot(part, part))
        send_core(cp, d, nt_dot(part, rows[...]))

    def over_chip(cp, d):
        settle(uc.at[cp, d], ucr_sem.at[cp, d])
        total = (us[cp, d] + uc[cp, d]).astype(jnp.bfloat16)
        for h in range(2):
            ux[cp, d, x * NC + h] = total[HALF * h : HALF * h + HALF]
        mine = ux.at[cp, d, me_t]
        for o in (2, 1, 3):
            for cc in range(NC):
                send(mine, mine, uxs_sem.at[cp], uxr_sem.at[cp, d], dev_t(((x + o) % NX) * NC + cc))

    def tokens_done(cp, d, first):
        settle(kbuf.at[cp, d, pl.ds(0, NT - 1)], kr_sem.at[cp, d])
        packed = kbuf[cp, d, 0]
        for t in range(1, NT):
            packed = packed + kbuf[cp, d, t]
        gram = jnp.concatenate([packed[:, R * j : R * j + R] for j in range(R // 8)], axis=0)
        inverse = invert_factor(gram)
        if first:
            row = lax.broadcasted_iota(jnp.int32, (R, R), 0)
            col = lax.broadcasted_iota(jnp.int32, (R, R), 1)
            identity = jnp.where(row == col, 1.0, 0.0)
            inverse = jnp.where(jnp.full((R, R), d) == 0, identity, inverse)
        settle(ux.at[cp, d, pl.ds(0, (NX - 1) * NC)], uxr_sem.at[cp, d])
        halves = []
        for h in range(2):
            total = ux[cp, d, h].astype(jnp.float32)
            for xx in range(1, NX):
                total = total + ux[cp, d, xx * NC + h].astype(jnp.float32)
            halves.append(total)
        total = jnp.concatenate(halves, axis=0)
        return inverse, nn_dot(inverse, total, lax.Precision.HIGHEST).astype(jnp.bfloat16)

    def scatter_wide(w, d, tok, rows):
        @pl.when(d > 0)
        def _():
            last_wide(w)

        for o in (2, 1, 3, 0):
            kk = (z // 2 + o) % GROUPS
            at = pl.ds(pl.multiple_of(kk * cols, LANES), cols)
            part = nn_dot(tok, rows[:, at]).astype(jnp.bfloat16)
            for h in range(2):
                for yy in range(NY):
                    for i in range(span + 1):
                        lo = (yy * span + i) * LANES
                        ysend[w, d, (2 * kk + h) * NY + yy, i] = part[
                            HALF * h : HALF * h + HALF, lo : lo + LANES
                        ]
            for h in range(2):
                zd = 2 * kk + h
                for q in (2, 1, 3):
                    yd = (y + q) % NY
                    send(
                        ysend.at[w, d, zd * NY + yd], yrecv.at[w, d, zd, q - 1],
                        ys_sem.at[w], yr_sem.at[w, zd], dev_dp(z, yd),
                    )

    def reduce_wide(w, d):
        for o in FAR + (0,):
            zd = (z + o) % NZ
            settle(yrecv.at[w, d, zd], yr_sem.at[w, zd])
            total = ysend[w, d, zd * NY + y].astype(jnp.float32)
            for q in range(NY - 1):
                total = total + yrecv[w, d, zd, q].astype(jnp.float32)
            if o:
                zsend[w, d, zd] = total.astype(jnp.bfloat16)
                send(
                    zsend.at[w, d, zd], zrecv.at[w, d, o - 1],
                    zs_sem.at[w], zr_sem.at[w], dev_dp(zd, y),
                )
            else:
                zown[w] = total

    def to_y(w, panel, i, zs):
        piece = panel.at[i, zs * NY + y]
        for q in (2, 1, 3):
            send(piece, piece, ag_sem.at[w], agy_sem.at[w, zs // 2], dev_dp(z, (y + q) % NY))

    def gather_wide(w, d, panel, i):
        settle(zrecv.at[w, d], zr_sem.at[w])
        total = zown[w]
        for q in range(NZ - 1):
            total = total + zrecv[w, d, q].astype(jnp.float32)
        panel[i, slot] = total.astype(jnp.bfloat16)
        piece = panel.at[i, slot]
        for o in NEAR:
            send(piece, piece, ag_sem.at[w], agz_sem.at[w, o - 1], dev_dp((z + o) % NZ, y))
        to_y(w, panel, i, z)

    def forward_wide(w, panel, i, offsets):
        for o in offsets:
            zs = (z + NZ - o) % NZ
            settle(panel.at[i, zs * NY + y], agz_sem.at[w, o - 1])
            to_y(w, panel, i, zs)

    def direct(src, dst, send_sem, recv_sem):
        for o in FAR + (0,):
            for q in (2, 1, 3, 0):
                if o or q:
                    zd, yd = (z + o) % NZ, (y + q) % NY
                    send(src(zd * NY + yd), dst, send_sem, recv_sem, dev_dp(zd, yd))

    def scatter_narrow(w, d, tok, rows):
        @pl.when(d > 0)
        def _():
            last_narrow(w)

        part = nn_dot(tok, rows[...]).astype(jnp.bfloat16)
        for t in range(SLOTS // 2):
            k, yy = t // NY, t % NY
            for h in range(2):
                nsend[w, d, (2 * k + h) * NY + yy] = part[
                    HALF * h : HALF * h + HALF, t * LANES : (t + 1) * LANES
                ]
        direct(lambda s: nsend.at[w, d, s], nrecv.at[w, d, slot], ns_sem.at[w], nr_sem.at[w])

    def gather_narrow(w, d, panel, i):
        settle(nrecv.at[w, d, pl.ds(0, SLOTS - 1)], nr_sem.at[w])
        nrecv[w, d, slot] = nsend[w, d, slot]
        total = nrecv[w, d, 0].astype(jnp.float32)
        for s in range(1, SLOTS):
            total = total + nrecv[w, d, s].astype(jnp.float32)
        panel[i, slot] = total.astype(jnp.bfloat16)
        piece = panel.at[i, slot]
        direct(lambda s: piece, piece, nag_sem.at[w], nagr_sem.at[w])

    def orthonormal(inverse, part):
        return nn_dot(inverse, part.astype(jnp.float32), lax.Precision.HIGHEST).astype(jnp.bfloat16)

    def pair(d, _):
        sums_narrow(2, d, dn_narrow, 1, gd_v, False)
        sums_wide(0, d, up_wide, 0, gu_v, False)
        over_chip(2, d)
        over_chip(0, d)

        @pl.when(d == 0)
        def _():
            loads[4].wait()
            loads[5].wait()

        _, tok = tokens_done(2, d, True)
        scatter_wide(1, d, tok, h_v)
        _, tok = tokens_done(0, d, True)
        scatter_narrow(0, d, tok, x_v)
        reduce_wide(1, d)
        gather_narrow(0, d, up_narrow, d)
        gather_wide(1, d, dn_wide, d)
        sums_narrow(1, d, up_narrow, 0, x_v, True)
        forward_wide(1, dn_wide, d, NEAR[:4])
        over_chip(1, d)
        forward_wide(1, dn_wide, d, NEAR[4:])
        inverse, tok = tokens_done(1, d, False)
        scatter_wide(0, d, tok, gu_v)

        @pl.when(d == PAIRS - 1)
        def _():
            qn_v[...] = orthonormal(inverse, narrow_all(up_narrow, d))
            pltpu.make_async_copy(qn_v, up_q, out_sem.at[0]).start()

        sums_wide(3, d, dn_wide, 1, h_v, True)
        over_chip(3, d)
        reduce_wide(0, d)
        inverse, tok = tokens_done(3, d, False)
        scatter_narrow(1, d, tok, gd_v)

        @pl.when(d == PAIRS - 1)
        def _():
            for k in range(GROUPS):
                qw_v[:, k * cols : (k + 1) * cols] = orthonormal(inverse, wide_group(dn_wide, d, k))
            pltpu.make_async_copy(qw_v, down_q, out_sem.at[1]).start()

        gather_wide(0, d, up_wide, d + 1)
        forward_wide(0, up_wide, d + 1, NEAR[:4])
        gather_narrow(1, d, dn_narrow, d + 1)
        forward_wide(0, up_wide, d + 1, NEAR[4:])
        return 0

    lax.fori_loop(0, PAIRS, pair, 0)

    wait_narrow(1)
    down_out = pltpu.make_async_copy(dn_narrow.at[PAIRS], down_img, out_sem.at[2])
    down_out.start()
    for k in range(GROUPS):
        wait_wide(0, k)
    up_out = pltpu.make_async_copy(up_wide.at[PAIRS], up_img, out_sem.at[3])
    up_out.start()
    for cp in range(4):
        last_tensor(cp)
    for w in range(2):
        last_wide(w)
        last_narrow(w)
    pltpu.make_async_copy(qn_v, up_q, out_sem.at[0]).wait()
    pltpu.make_async_copy(qw_v, down_q, out_sem.at[1]).wait()
    down_out.wait()
    up_out.wait()


def finish(scales, up_q, up_img, down_q, down_img, up_a, up_b, down_a, down_b):
    up_scale, down_scale, scale = scales
    up_a[...] = up_q[...].astype(jnp.float32) * up_scale
    down_a[...] = down_q[...].astype(jnp.float32) * down_scale
    tiles = up_b.shape[1] // LANES // GROUPS
    span = tiles // NY
    for k in range(GROUPS):
        for h in range(2):
            rows = slice(HALF * h, HALF * h + HALF)
            for t in range(tiles):
                yy = min(t // span, NY - 1)
                lo = (k * tiles + t) * LANES
                piece = up_img[(2 * k + h) * NY + yy, t - span * yy]
                up_b[rows, lo : lo + LANES] = piece.astype(jnp.float32) * scale
            for yy in range(NY):
                lo = (k * NY + yy) * LANES
                piece = down_img[(2 * k + h) * NY + yy]
                down_b[rows, lo : lo + LANES] = piece.astype(jnp.float32) * scale


def local(x_in, grad_up, hidden_act, grad_down, sketch_up, sketch_down):
    tokens, n_narrow = x_in.shape
    n_wide = grad_up.shape[1]
    tail = (HALF, LANES)
    piece = (n_wide // LANES // GROUPS // NY + 1,) + tail
    bf16, f32 = jnp.bfloat16, jnp.float32
    dma = pltpu.SemaphoreType.DMA
    vmem = pltpu.VMEM
    scratch = [
        vmem((tokens, n_narrow), bf16),
        vmem((tokens, n_wide), bf16),
        vmem((tokens, n_wide), bf16),
        vmem((tokens, n_narrow), bf16),
        vmem((R, n_wide), bf16),
        vmem((R, n_narrow), bf16),
        vmem((R, n_narrow), bf16),
        vmem((R, n_wide), bf16),
        vmem((PAIRS + 1, SLOTS) + piece, bf16),
        vmem((PAIRS, SLOTS) + tail, bf16),
        vmem((PAIRS, SLOTS) + piece, bf16),
        vmem((PAIRS + 1, SLOTS) + tail, bf16),
        vmem((2, PAIRS, SLOTS) + piece, bf16),
        vmem((2, PAIRS, NZ, NY - 1) + piece, bf16),
        vmem((2,) + piece, f32),
        vmem((2, PAIRS, NZ) + piece, bf16),
        vmem((2, PAIRS, NZ - 1) + piece, bf16),
        vmem((2, PAIRS, SLOTS) + tail, bf16),
        vmem((2, PAIRS, SLOTS) + tail, bf16),
        vmem((4, PAIRS, R, tokens), f32),
        vmem((4, PAIRS, R, tokens), f32),
        vmem((4, PAIRS, NT, HALF, tokens), bf16),
        vmem((GROUPS, R, R), f32),
        vmem((4, PAIRS, NT, 8, LANES), f32),
        dma((6,)), dma((4,)), dma((2,)), dma((2, NZ)), dma((2,)), dma((2,)),
        dma((2,)), dma((2, NZ - 1)), dma((2, GROUPS)),
        dma((2,)), dma((2,)), dma((2,)), dma((2,)),
        dma((4,)), dma((4, PAIRS)), dma((4,)), dma((4, PAIRS)), dma((4,)), dma((4, PAIRS)),
    ]
    panels = pl.pallas_call(
        kernel,
        out_shape=(
            jax.ShapeDtypeStruct((R, n_narrow), bf16),
            jax.ShapeDtypeStruct((SLOTS,) + piece, bf16),
            jax.ShapeDtypeStruct((R, n_wide), bf16),
            jax.ShapeDtypeStruct((SLOTS,) + tail, bf16),
        ),
        in_specs=[pl.BlockSpec(memory_space=pl.ANY)] * 6,
        out_specs=[pl.BlockSpec(memory_space=pl.ANY)] * 4,
        scratch_shapes=scratch,
        compiler_params=pltpu.CompilerParams(
            collective_id=0, has_side_effects=True, vmem_limit_bytes=56 * 2**20
        ),
    )(x_in, grad_up, hidden_act, grad_down, sketch_up, sketch_down)
    width = lax.axis_size("tensor")
    scales = (
        math.sqrt(n_narrow * width),
        math.sqrt(n_wide * width),
        1.0 / math.sqrt(tokens * lax.axis_size("dp")),
    )
    return pl.pallas_call(
        functools.partial(finish, scales),
        out_shape=(
            jax.ShapeDtypeStruct((R, n_narrow), f32),
            jax.ShapeDtypeStruct((R, n_wide), f32),
            jax.ShapeDtypeStruct((R, n_wide), f32),
            jax.ShapeDtypeStruct((R, n_narrow), f32),
        ),
        in_specs=[pl.BlockSpec(memory_space=pltpu.VMEM)] * 4,
        out_specs=[pl.BlockSpec(memory_space=pltpu.VMEM)] * 4,
        compiler_params=pltpu.CompilerParams(vmem_limit_bytes=16 * 2**20),
    )(*panels)


def solution(mesh):
    in_specs = (
        P("dp", "tensor"),
        P("dp", "tensor"),
        P("dp", "tensor"),
        P("dp", "tensor"),
        P(None, "tensor"),
        P(None, "tensor"),
    )
    out_specs = (P(None, "tensor"), P(None, "tensor"), P(None, "tensor"), P(None, "tensor"))
    return jax.shard_map(local, mesh=mesh, in_specs=in_specs, out_specs=out_specs, check_vma=False)
```

```python
import functools
import math

import jax
import jax.numpy as jnp
from jax import lax
from jax.experimental import pallas as pl
from jax.experimental.pallas import tpu as pltpu
from jax.sharding import PartitionSpec as P

MESH = pl.DeviceIdType.MESH

NZ, NY, NX, NC = 8, 4, 4, 2
R = 32
ITERS = 2
PAIRS = ITERS + 1
HALF = R // 2
LANES = 128
GROUPS = NZ // 2
SLOTS = NZ * NY
NT = NX * NC
BLOCK = 16

FAR = (4, 3, 5, 2, 6, 1, 7)
NEAR = (1, 7, 2, 6, 3, 5, 4)


def nt_dot(a, b):
    return lax.dot_general(a, b, (((1,), (1,)), ((), ())), preferred_element_type=jnp.float32)


def nn_dot(a, b, precision=None):
    return lax.dot_general(
        a, b, (((1,), (0,)), ((), ())), precision=precision, preferred_element_type=jnp.float32
    )


def invert_factor(gram):
    lane = lax.broadcasted_iota(jnp.int32, (R, LANES), 1)
    row = lax.broadcasted_iota(jnp.int32, (R, LANES), 0)
    right = lane >= R
    padded = jnp.concatenate([gram, jnp.zeros((R, LANES - R), jnp.float32)], axis=1)
    work = jnp.where(right, jnp.where(lane - R == row, 1.0, 0.0), padded)
    scale = jnp.zeros((R, LANES), jnp.float32)
    for b in range(0, R, BLOCK):
        cols = [jnp.broadcast_to(work[:, b + j : b + j + 1], (R, LANES)) for j in range(BLOCK)]
        for j in range(BLOCK):
            k = b + j
            pivot = jnp.broadcast_to(cols[j][k : k + 1, :], (R, LANES))
            scale = jnp.where(row == k, lax.rsqrt(pivot), scale)
            factor = jnp.where(row > k, cols[j] * (1.0 / pivot), 0.0)
            for i in range(j + 1, BLOCK):
                cols[i] = cols[i] - factor * jnp.broadcast_to(cols[i][k : k + 1, :], (R, LANES))
            work = work - factor * jnp.broadcast_to(work[k : k + 1, :], (R, LANES))
    return (work * scale)[:, R : 2 * R]


def place(t, span, k):
    row = min(t // span, NY - 1)
    if t % span or row == 0 or t // span > row:
        return row, t - span * row
    if isinstance(k, int):
        return (row - 1, span) if row > k else (row, 0)
    return jnp.where(row > k, row - 1, row), jnp.where(row > k, span, 0)


def settle(ref, sem):
    pltpu.make_async_copy(ref, ref, sem).wait()


def kernel(
    x_in, grad_up, hidden_act, grad_down, sketch_up, sketch_down,
    up_q, up_img, down_q, down_img,
    x_v, gu_v, h_v, gd_v, sk_wide, sk_narrow, qn_v, qw_v,
    up_wide, up_narrow, dn_wide, dn_narrow,
    ysend, yrecv, zown, zsend, zrecv, nsend, nrecv,
    ux, kparts, kbuf,
    in_sem, out_sem, ys_sem, yr_sem, zs_sem, zr_sem, ag_sem, agz_sem, agy_sem,
    ns_sem, nr_sem, nag_sem, nagr_sem, ks_sem, kr_sem, uxs_sem, uxr_sem,
    ysx_sem, yx_sem, zsx_sem, zx_sem, agx_sem, agzs_sem, agzx_sem, agyx_sem,
):
    dp = lax.axis_index("dp")
    me_t = lax.axis_index("tensor")
    z, y = dp // NY, dp % NY
    x, c = me_t // NC, me_t % NC
    slot = dp
    n_wide, n_narrow = gu_v.shape[1], x_v.shape[1]
    tiles = n_wide // LANES // GROUPS
    span = tiles // NY
    cols = tiles * LANES
    tokens = gu_v.shape[0]

    loads = [
        pltpu.make_async_copy(src, dst, in_sem.at[i])
        for i, (src, dst) in enumerate(
            (
                (sketch_down, sk_narrow),
                (sketch_up, sk_wide),
                (grad_down, gd_v),
                (grad_up, gu_v),
                (hidden_act, h_v),
                (x_in, x_v),
            )
        )
    ]
    for load in loads:
        load.start()

    def dev_dp(zz, yy):
        return (zz * NY + yy, me_t)

    def dev_t(tt):
        return (dp, tt)

    def send(src, dst, send_sem, recv_sem, device):
        pltpu.make_async_remote_copy(
            src, dst, send_sem, recv_sem, device_id=device, device_id_type=MESH
        ).start()

    barrier = pltpu.get_barrier_semaphore()
    peers = [((dp + o) % SLOTS, me_t) for o in range(1, SLOTS)]
    peers += [dev_t((me_t + o) % NT) for o in range(1, NT)]
    for peer in peers:
        pl.semaphore_signal(barrier, inc=1, device_id=peer, device_id_type=MESH)

    for load in loads[:4]:
        load.wait()

    for k in range(GROUPS):
        for h in range(2):
            rows = slice(HALF * h, HALF * h + HALF)
            for yy in range(NY):
                s = (2 * k + h) * NY + yy
                for i in range(span + 1):
                    lo = (k * tiles + yy * span + i) * LANES
                    up_wide[0, s, i] = sk_wide[rows, lo : lo + LANES]
                lo = (k * NY + yy) * LANES
                dn_narrow[0, s] = sk_narrow[rows, lo : lo + LANES]

    pl.semaphore_wait(barrier, len(peers))

    def core_part(yy, kk):
        return pl.ds(jnp.where(yy > kk, 1, 0), span)

    last_part = pl.ds(span, 1)

    def wide_group(panel, i, kk):
        out = []
        for t in range(tiles):
            yy, n = place(t, span, kk)
            out.append(
                jnp.concatenate([panel[i, (2 * kk + h) * NY + yy, n] for h in range(2)], axis=0)
            )
        return jnp.concatenate(out, axis=1)

    def narrow_all(panel, i):
        out = []
        for t in range(SLOTS // 2):
            k, yy = t // NY, t % NY
            out.append(
                jnp.concatenate([panel[i, (2 * k + h) * NY + yy] for h in range(2)], axis=0)
            )
        return jnp.concatenate(out, axis=1)

    def send_gram(cp, d, gram):
        packed = jnp.concatenate([gram[8 * j : 8 * j + 8, :] for j in range(R // 8)], axis=1)
        kbuf[cp, d, me_t] = packed
        mine = kbuf.at[cp, d, me_t]
        for o in (1, 2, 3, 4, 5, 6, 7):
            send(mine, mine, ks_sem.at[cp], kr_sem.at[cp, d], dev_t((me_t + o) % NT))

    def send_sums(cp, d, total):
        ux[cp, d, me_t] = total.astype(jnp.bfloat16)
        mine = ux.at[cp, d, me_t]
        for o in (4, 3, 5, 2, 6, 1, 7):
            send(mine, mine, uxs_sem.at[cp], uxr_sem.at[cp, d], dev_t((me_t + o) % NT))

    def past_sends(cp, d):
        @pl.when(d > 0)
        def _():
            last_tensor(cp)

    def last_tensor(cp):
        settle(kbuf.at[cp, 0, pl.ds(0, NT - 1)], ks_sem.at[cp])
        settle(ux.at[cp, 0, pl.ds(0, NT - 1)], uxs_sem.at[cp])

    def last_wide(w):
        settle(ysend.at[w, 0, pl.ds(0, NZ * (NY - 1)), pl.ds(0, span)], ys_sem.at[w])
        settle(ysend.at[w, 0, pl.ds(0, 2 * (GROUPS - 1)), last_part], ysx_sem.at[w])
        settle(zsend.at[w, 0, pl.ds(0, NZ - 1), pl.ds(0, span)], zs_sem.at[w])
        settle(up_wide.at[0, pl.ds(0, SLOTS - 1), pl.ds(0, span)], ag_sem.at[w])
        settle(up_wide.at[0, pl.ds(0, 2 * (NY - 1)), last_part], agx_sem.at[w])
        for h in range(2):

            @pl.when(z != 2 * y + h)
            def _():
                settle(zsend.at[w, 0, h, last_part], zsx_sem.at[w, h])

        @pl.when(z // 2 == y)
        def _():
            settle(up_wide.at[0, pl.ds(0, NZ - 1), last_part], agzs_sem.at[w])

    def last_narrow(w):
        settle(nsend.at[w, 0, pl.ds(0, SLOTS - 1)], ns_sem.at[w])
        settle(up_narrow.at[0, pl.ds(0, SLOTS - 1)], nag_sem.at[w])

    def wait_wide(w, kk):
        settle(up_wide.at[0, pl.ds(0, 2 * (NY - 1)), pl.ds(0, span)], agy_sem.at[w, kk])

        @pl.when(kk != y)
        def _():
            settle(up_wide.at[0, pl.ds(0, 2), last_part], agyx_sem.at[w, kk])

    def wait_narrow(w):
        settle(up_narrow.at[0, pl.ds(0, SLOTS - 1)], nagr_sem.at[w])

    def sums_wide(cp, d, panel, w, rows, fresh):
        past_sends(cp, d)
        total = jnp.zeros((R, tokens), jnp.float32)
        for n, o in enumerate((0, 1, 3, 2)):
            kk = (z // 2 + o) % GROUPS
            if fresh:
                wait_wide(w, kk)
            else:

                @pl.when(d > 0)
                def _():
                    wait_wide(w, kk)

            part = wide_group(panel, d, kk)
            kparts[kk] = nt_dot(part, part)
            if n == GROUPS - 1:
                send_gram(cp, d, ((kparts[0] + kparts[1]) + kparts[2]) + kparts[3])
            at = pl.ds(pl.multiple_of(kk * cols, LANES), cols)
            total = total + nt_dot(part, rows[:, at])
        send_sums(cp, d, total)

    def sums_narrow(cp, d, panel, w, rows, fresh):
        past_sends(cp, d)
        if fresh:
            wait_narrow(w)
        else:

            @pl.when(d > 0)
            def _():
                wait_narrow(w)

        part = narrow_all(panel, d)
        send_gram(cp, d, nt_dot(part, part))
        send_sums(cp, d, nt_dot(part, rows[...]))

    def tokens_done(cp, d, first):
        settle(kbuf.at[cp, d, pl.ds(0, NT - 1)], kr_sem.at[cp, d])
        packed = kbuf[cp, d, 0]
        for t in range(1, NT):
            packed = packed + kbuf[cp, d, t]
        gram = jnp.concatenate([packed[:, R * j : R * j + R] for j in range(R // 8)], axis=0)
        inverse = invert_factor(gram)
        if first:
            row = lax.broadcasted_iota(jnp.int32, (R, R), 0)
            col = lax.broadcasted_iota(jnp.int32, (R, R), 1)
            identity = jnp.where(row == col, 1.0, 0.0)
            inverse = jnp.where(jnp.full((R, R), d) == 0, identity, inverse)
        settle(ux.at[cp, d, pl.ds(0, NT - 1)], uxr_sem.at[cp, d])
        total = ux[cp, d, 0].astype(jnp.float32)
        for t in range(1, NT):
            total = total + ux[cp, d, t].astype(jnp.float32)
        return inverse, nn_dot(inverse, total, lax.Precision.HIGHEST).astype(jnp.bfloat16)

    def scatter_wide(w, d, tok, rows):
        @pl.when(d > 0)
        def _():
            last_wide(w)

        for o in (2, 1, 3, 0):
            kk = (z // 2 + o) % GROUPS
            at = pl.ds(pl.multiple_of(kk * cols, LANES), cols)
            part = nn_dot(tok, rows[:, at]).astype(jnp.bfloat16)
            for h in range(2):
                for yy in range(NY):
                    for i in range(span + 1):
                        lo = (yy * span + i) * LANES
                        ysend[w, d, (2 * kk + h) * NY + yy, i] = part[
                            HALF * h : HALF * h + HALF, lo : lo + LANES
                        ]
            for h in range(2):
                zd = 2 * kk + h
                for q in (2, 1, 3):
                    yd = (y + q) % NY
                    part = core_part(yd, kk)
                    send(
                        ysend.at[w, d, zd * NY + yd, part], yrecv.at[w, d, zd, q - 1, part],
                        ys_sem.at[w], yr_sem.at[w, zd], dev_dp(z, yd),
                    )

            @pl.when(kk != y)
            def _():
                for h in range(2):
                    zd = 2 * kk + h
                    q = (kk + NY - y) % NY
                    send(
                        ysend.at[w, d, zd * NY + kk, last_part],
                        yrecv.at[w, d, zd, q - 1, last_part],
                        ysx_sem.at[w], yx_sem.at[w, h], dev_dp(z, kk),
                    )

    def reduce_wide(w, d):
        for o in FAR + (0,):
            zd = (z + o) % NZ
            settle(yrecv.at[w, d, zd, pl.ds(0, NY - 1), pl.ds(0, span)], yr_sem.at[w, zd])

            @pl.when(zd // 2 == y)
            def _():
                settle(yrecv.at[w, d, zd, pl.ds(0, NY - 1), last_part], yx_sem.at[w, zd % 2])

            total = ysend[w, d, zd * NY + y].astype(jnp.float32)
            for q in range(NY - 1):
                total = total + yrecv[w, d, zd, q].astype(jnp.float32)
            if o:
                zsend[w, d, zd] = total.astype(jnp.bfloat16)
                part = core_part(y, zd // 2)
                send(
                    zsend.at[w, d, zd, part], zrecv.at[w, d, o - 1, part],
                    zs_sem.at[w], zr_sem.at[w], dev_dp(zd, y),
                )

                @pl.when(zd // 2 == y)
                def _():
                    send(
                        zsend.at[w, d, zd, last_part], zrecv.at[w, d, o - 1, last_part],
                        zsx_sem.at[w, zd % 2], zx_sem.at[w], dev_dp(zd, y),
                    )

            else:
                zown[w] = total

    def to_y(w, panel, i, zs):
        s = zs * NY + y
        piece = panel.at[i, s, core_part(y, zs // 2)]
        for q in (2, 1, 3):
            send(piece, piece, ag_sem.at[w], agy_sem.at[w, zs // 2], dev_dp(z, (y + q) % NY))

        @pl.when(zs // 2 == y)
        def _():
            last = panel.at[i, s, last_part]
            for q in (2, 1, 3):
                send(last, last, agx_sem.at[w], agyx_sem.at[w, zs // 2], dev_dp(z, (y + q) % NY))

    def gather_wide(w, d, panel, i):
        settle(zrecv.at[w, d, pl.ds(0, NZ - 1), pl.ds(0, span)], zr_sem.at[w])

        @pl.when(z // 2 == y)
        def _():
            settle(zrecv.at[w, d, pl.ds(0, NZ - 1), last_part], zx_sem.at[w])

        total = zown[w]
        for q in range(NZ - 1):
            total = total + zrecv[w, d, q].astype(jnp.float32)
        panel[i, slot] = total.astype(jnp.bfloat16)
        piece = panel.at[i, slot, core_part(y, z // 2)]
        for o in NEAR:
            send(piece, piece, ag_sem.at[w], agz_sem.at[w, o - 1], dev_dp((z + o) % NZ, y))

        @pl.when(z // 2 == y)
        def _():
            last = panel.at[i, slot, last_part]
            for o in NEAR:
                send(last, last, agzs_sem.at[w], agzx_sem.at[w, o - 1], dev_dp((z + o) % NZ, y))

        to_y(w, panel, i, z)

    def forward_wide(w, panel, i):
        for o in NEAR:
            zs = (z + NZ - o) % NZ
            settle(panel.at[i, zs * NY + y, pl.ds(0, span)], agz_sem.at[w, o - 1])

            @pl.when(zs // 2 == y)
            def _():
                settle(panel.at[i, zs * NY + y, last_part], agzx_sem.at[w, o - 1])

            to_y(w, panel, i, zs)

    def direct(src, dst, send_sem, recv_sem):
        for o in FAR + (0,):
            for q in (2, 1, 3, 0):
                if o or q:
                    zd, yd = (z + o) % NZ, (y + q) % NY
                    send(src(zd * NY + yd), dst, send_sem, recv_sem, dev_dp(zd, yd))

    def scatter_narrow(w, d, tok, rows):
        @pl.when(d > 0)
        def _():
            last_narrow(w)

        part = nn_dot(tok, rows[...]).astype(jnp.bfloat16)
        for t in range(SLOTS // 2):
            k, yy = t // NY, t % NY
            for h in range(2):
                nsend[w, d, (2 * k + h) * NY + yy] = part[
                    HALF * h : HALF * h + HALF, t * LANES : (t + 1) * LANES
                ]
        direct(lambda s: nsend.at[w, d, s], nrecv.at[w, d, slot], ns_sem.at[w], nr_sem.at[w])

    def gather_narrow(w, d, panel, i):
        settle(nrecv.at[w, d, pl.ds(0, SLOTS - 1)], nr_sem.at[w])
        nrecv[w, d, slot] = nsend[w, d, slot]
        total = nrecv[w, d, 0].astype(jnp.float32)
        for s in range(1, SLOTS):
            total = total + nrecv[w, d, s].astype(jnp.float32)
        panel[i, slot] = total.astype(jnp.bfloat16)
        piece = panel.at[i, slot]
        direct(lambda s: piece, piece, nag_sem.at[w], nagr_sem.at[w])

    def orthonormal(inverse, part):
        return nn_dot(inverse, part.astype(jnp.float32), lax.Precision.HIGHEST).astype(jnp.bfloat16)

    def pair(d, _):
        sums_narrow(2, d, dn_narrow, 1, gd_v, False)
        sums_wide(0, d, up_wide, 0, gu_v, False)

        @pl.when(d == 0)
        def _():
            loads[4].wait()
            loads[5].wait()

        _, tok = tokens_done(2, d, True)
        scatter_wide(1, d, tok, h_v)
        _, tok = tokens_done(0, d, True)
        scatter_narrow(0, d, tok, x_v)
        reduce_wide(1, d)
        gather_narrow(0, d, up_narrow, d)
        gather_wide(1, d, dn_wide, d)
        forward_wide(1, dn_wide, d)
        sums_narrow(1, d, up_narrow, 0, x_v, True)
        sums_wide(3, d, dn_wide, 1, h_v, True)
        inverse, tok = tokens_done(1, d, False)
        scatter_wide(0, d, tok, gu_v)

        @pl.when(d == PAIRS - 1)
        def _():
            qn_v[...] = orthonormal(inverse, narrow_all(up_narrow, d))
            pltpu.make_async_copy(qn_v, up_q, out_sem.at[0]).start()

        inverse, tok = tokens_done(3, d, False)
        scatter_narrow(1, d, tok, gd_v)

        @pl.when(d == PAIRS - 1)
        def _():
            for k in range(GROUPS):
                qw_v[:, k * cols : (k + 1) * cols] = orthonormal(inverse, wide_group(dn_wide, d, k))
            pltpu.make_async_copy(qw_v, down_q, out_sem.at[1]).start()

        reduce_wide(0, d)
        gather_wide(0, d, up_wide, d + 1)
        gather_narrow(1, d, dn_narrow, d + 1)
        forward_wide(0, up_wide, d + 1)
        return 0

    lax.fori_loop(0, PAIRS, pair, 0)

    wait_narrow(1)
    down_out = pltpu.make_async_copy(dn_narrow.at[PAIRS], down_img, out_sem.at[2])
    down_out.start()
    for k in range(GROUPS):
        wait_wide(0, k)
    up_out = pltpu.make_async_copy(up_wide.at[PAIRS], up_img, out_sem.at[3])
    up_out.start()
    for cp in range(4):
        last_tensor(cp)
    for w in range(2):
        last_wide(w)
        last_narrow(w)
    pltpu.make_async_copy(qn_v, up_q, out_sem.at[0]).wait()
    pltpu.make_async_copy(qw_v, down_q, out_sem.at[1]).wait()
    down_out.wait()
    up_out.wait()


def finish(scales, up_q, up_img, down_q, down_img, up_a, up_b, down_a, down_b, uq, ui, dq, di, ua, ub, da, db, sem):
    up_scale, down_scale, scale = scales
    loads = [
        pltpu.make_async_copy(src, dst, sem.at[i])
        for i, (src, dst) in enumerate(((up_q, uq), (down_q, dq), (down_img, di), (up_img, ui)))
    ]
    for load in loads:
        load.start()
    stores = [
        pltpu.make_async_copy(src, dst, sem.at[4 + i])
        for i, (src, dst) in enumerate(((ua, up_a), (da, down_a), (db, down_b), (ub, up_b)))
    ]
    loads[0].wait()
    ua[...] = uq[...].astype(jnp.float32) * up_scale
    stores[0].start()
    loads[1].wait()
    da[...] = dq[...].astype(jnp.float32) * down_scale
    stores[1].start()
    tiles = ub.shape[1] // LANES // GROUPS
    span = tiles // NY
    loads[2].wait()
    for k in range(GROUPS):
        for h in range(2):
            for yy in range(NY):
                lo = (k * NY + yy) * LANES
                piece = di[(2 * k + h) * NY + yy]
                db[HALF * h : HALF * h + HALF, lo : lo + LANES] = piece.astype(jnp.float32) * scale
    stores[2].start()
    loads[3].wait()
    for k in range(GROUPS):
        for h in range(2):
            for t in range(tiles):
                yy, n = place(t, span, k)
                lo = (k * tiles + t) * LANES
                piece = ui[(2 * k + h) * NY + yy, n]
                ub[HALF * h : HALF * h + HALF, lo : lo + LANES] = piece.astype(jnp.float32) * scale
    stores[3].start()
    for store in stores:
        store.wait()


def local(x_in, grad_up, hidden_act, grad_down, sketch_up, sketch_down):
    tokens, n_narrow = x_in.shape
    n_wide = grad_up.shape[1]
    tail = (HALF, LANES)
    piece = (n_wide // LANES // GROUPS // NY + 1,) + tail
    bf16, f32 = jnp.bfloat16, jnp.float32
    dma = pltpu.SemaphoreType.DMA
    vmem = pltpu.VMEM
    scratch = [
        vmem((tokens, n_narrow), bf16),
        vmem((tokens, n_wide), bf16),
        vmem((tokens, n_wide), bf16),
        vmem((tokens, n_narrow), bf16),
        vmem((R, n_wide), bf16),
        vmem((R, n_narrow), bf16),
        vmem((R, n_narrow), bf16),
        vmem((R, n_wide), bf16),
        vmem((PAIRS + 1, SLOTS) + piece, bf16),
        vmem((PAIRS, SLOTS) + tail, bf16),
        vmem((PAIRS, SLOTS) + piece, bf16),
        vmem((PAIRS + 1, SLOTS) + tail, bf16),
        vmem((2, PAIRS, SLOTS) + piece, bf16),
        vmem((2, PAIRS, NZ, NY - 1) + piece, bf16),
        vmem((2,) + piece, f32),
        vmem((2, PAIRS, NZ) + piece, bf16),
        vmem((2, PAIRS, NZ - 1) + piece, bf16),
        vmem((2, PAIRS, SLOTS) + tail, bf16),
        vmem((2, PAIRS, SLOTS) + tail, bf16),
        vmem((4, PAIRS, NT, R, tokens), bf16),
        vmem((GROUPS, R, R), f32),
        vmem((4, PAIRS, NT, 8, LANES), f32),
        dma((6,)), dma((4,)), dma((2,)), dma((2, NZ)), dma((2,)), dma((2,)),
        dma((2,)), dma((2, NZ - 1)), dma((2, GROUPS)),
        dma((2,)), dma((2,)), dma((2,)), dma((2,)),
        dma((4,)), dma((4, PAIRS)), dma((4,)), dma((4, PAIRS)),
        dma((2,)), dma((2, 2)), dma((2, 2)), dma((2,)),
        dma((2,)), dma((2,)), dma((2, NZ - 1)), dma((2, GROUPS)),
    ]
    panels = pl.pallas_call(
        kernel,
        out_shape=(
            jax.ShapeDtypeStruct((R, n_narrow), bf16),
            jax.ShapeDtypeStruct((SLOTS,) + piece, bf16),
            jax.ShapeDtypeStruct((R, n_wide), bf16),
            jax.ShapeDtypeStruct((SLOTS,) + tail, bf16),
        ),
        in_specs=[pl.BlockSpec(memory_space=pl.ANY)] * 6,
        out_specs=[pl.BlockSpec(memory_space=pl.ANY)] * 4,
        scratch_shapes=scratch,
        compiler_params=pltpu.CompilerParams(
            collective_id=0, has_side_effects=True, vmem_limit_bytes=56 * 2**20
        ),
    )(x_in, grad_up, hidden_act, grad_down, sketch_up, sketch_down)
    width = lax.axis_size("tensor")
    scales = (
        math.sqrt(n_narrow * width),
        math.sqrt(n_wide * width),
        1.0 / math.sqrt(tokens * lax.axis_size("dp")),
    )
    outs = (
        jax.ShapeDtypeStruct((R, n_narrow), f32),
        jax.ShapeDtypeStruct((R, n_wide), f32),
        jax.ShapeDtypeStruct((R, n_wide), f32),
        jax.ShapeDtypeStruct((R, n_narrow), f32),
    )
    return pl.pallas_call(
        functools.partial(finish, scales),
        out_shape=outs,
        in_specs=[pl.BlockSpec(memory_space=pl.ANY)] * 4,
        out_specs=[pl.BlockSpec(memory_space=pl.ANY)] * 4,
        scratch_shapes=[vmem(a.shape, a.dtype) for a in tuple(panels) + outs] + [dma((8,))],
        compiler_params=pltpu.CompilerParams(vmem_limit_bytes=56 * 2**20),
    )(*panels)


def solution(mesh):
    in_specs = (
        P("dp", "tensor"),
        P("dp", "tensor"),
        P("dp", "tensor"),
        P("dp", "tensor"),
        P(None, "tensor"),
        P(None, "tensor"),
    )
    out_specs = (P(None, "tensor"), P(None, "tensor"), P(None, "tensor"), P(None, "tensor"))
    return jax.shard_map(local, mesh=mesh, in_specs=in_specs, out_specs=out_specs, check_vma=False)
```

```python
import functools
import math

import jax
import jax.numpy as jnp
from jax import lax
from jax.experimental import pallas as pl
from jax.experimental.pallas import tpu as pltpu
from jax.sharding import PartitionSpec as P

MESH = pl.DeviceIdType.MESH

NZ, NY, NX, NC = 8, 4, 4, 2
R = 32
ITERS = 2
PAIRS = ITERS + 1
HALF = R // 2
LANES = 128
GROUPS = NZ // 2
SLOTS = NZ * NY
NT = NX * NC
BLOCK = 16

FAR = (4, 3, 5, 2, 6, 1, 7)
NEAR = (1, 7, 2, 6, 3, 5, 4)


def nt_dot(a, b):
    return lax.dot_general(a, b, (((1,), (1,)), ((), ())), preferred_element_type=jnp.float32)


def nn_dot(a, b, precision=None):
    return lax.dot_general(
        a, b, (((1,), (0,)), ((), ())), precision=precision, preferred_element_type=jnp.float32
    )


def invert_factor(gram):
    lane = lax.broadcasted_iota(jnp.int32, (R, LANES), 1)
    row = lax.broadcasted_iota(jnp.int32, (R, LANES), 0)
    right = lane >= R
    padded = jnp.concatenate([gram, jnp.zeros((R, LANES - R), jnp.float32)], axis=1)
    work = jnp.where(right, jnp.where(lane - R == row, 1.0, 0.0), padded)
    scale = jnp.zeros((R, LANES), jnp.float32)
    for b in range(0, R, BLOCK):
        cols = [jnp.broadcast_to(work[:, b + j : b + j + 1], (R, LANES)) for j in range(BLOCK)]
        for j in range(BLOCK):
            k = b + j
            pivot = jnp.broadcast_to(cols[j][k : k + 1, :], (R, LANES))
            scale = jnp.where(row == k, lax.rsqrt(pivot), scale)
            factor = jnp.where(row > k, cols[j] * (1.0 / pivot), 0.0)
            for i in range(j + 1, BLOCK):
                cols[i] = cols[i] - factor * jnp.broadcast_to(cols[i][k : k + 1, :], (R, LANES))
            work = work - factor * jnp.broadcast_to(work[k : k + 1, :], (R, LANES))
    return (work * scale)[:, R : 2 * R]


def place(t, span, k):
    row = min(t // span, NY - 1)
    if t % span or row == 0 or t // span > row:
        return row, t - span * row
    if isinstance(k, int):
        return (row - 1, span) if row > k else (row, 0)
    return jnp.where(row > k, row - 1, row), jnp.where(row > k, span, 0)


def settle(ref, sem):
    pltpu.make_async_copy(ref, ref, sem).wait()


def kernel(
    x_in, grad_up, hidden_act, grad_down, sketch_up, sketch_down,
    up_q, up_img, down_q, down_img,
    x_v, gu_v, h_v, gd_v, sk_wide, sk_narrow, qn_v, qw_v,
    up_wide, up_narrow, dn_wide, dn_narrow,
    ysend, yrecv, zown, zsend, zrecv, nsend, nrecv,
    ux, kparts, kbuf,
    in_sem, out_sem, ys_sem, yr_sem, zs_sem, zr_sem, ag_sem, agz_sem, agy_sem,
    ns_sem, nr_sem, nag_sem, nagr_sem, ks_sem, kr_sem, uxs_sem, uxr_sem,
    ysx_sem, yx_sem, zsx_sem, zx_sem, agx_sem, agzs_sem, agzx_sem, agyx_sem,
):
    dp = lax.axis_index("dp")
    me_t = lax.axis_index("tensor")
    z, y = dp // NY, dp % NY
    x, c = me_t // NC, me_t % NC
    slot = dp
    n_wide, n_narrow = gu_v.shape[1], x_v.shape[1]
    tiles = n_wide // LANES // GROUPS
    span = tiles // NY
    cols = tiles * LANES
    tokens = gu_v.shape[0]

    loads = [
        pltpu.make_async_copy(src, dst, in_sem.at[i])
        for i, (src, dst) in enumerate(
            (
                (sketch_down, sk_narrow),
                (sketch_up, sk_wide),
                (grad_down, gd_v),
                (grad_up, gu_v),
                (hidden_act, h_v),
                (x_in, x_v),
            )
        )
    ]
    for load in loads:
        load.start()

    def dev_dp(zz, yy):
        return (zz * NY + yy, me_t)

    def dev_t(tt):
        return (dp, tt)

    def send(src, dst, send_sem, recv_sem, device):
        pltpu.make_async_remote_copy(
            src, dst, send_sem, recv_sem, device_id=device, device_id_type=MESH
        ).start()

    barrier = pltpu.get_barrier_semaphore()
    peers = [((dp + o) % SLOTS, me_t) for o in range(1, SLOTS)]
    peers += [dev_t((me_t + o) % NT) for o in range(1, NT)]
    for peer in peers:
        pl.semaphore_signal(barrier, inc=1, device_id=peer, device_id_type=MESH)

    for load in loads[:4]:
        load.wait()

    for k in range(GROUPS):
        for h in range(2):
            rows = slice(HALF * h, HALF * h + HALF)
            for yy in range(NY):
                s = (2 * k + h) * NY + yy
                for i in range(span + 1):
                    lo = (k * tiles + yy * span + i) * LANES
                    up_wide[0, s, i] = sk_wide[rows, lo : lo + LANES]
                lo = (k * NY + yy) * LANES
                dn_narrow[0, s] = sk_narrow[rows, lo : lo + LANES]

    def core_part(yy, kk):
        return pl.ds(jnp.where(yy > kk, 1, 0), span)

    last_part = pl.ds(span, 1)

    def wide_group(panel, i, kk):
        out = []
        for t in range(tiles):
            yy, n = place(t, span, kk)
            out.append(
                jnp.concatenate([panel[i, (2 * kk + h) * NY + yy, n] for h in range(2)], axis=0)
            )
        return jnp.concatenate(out, axis=1)

    def narrow_all(panel, i):
        out = []
        for t in range(SLOTS // 2):
            k, yy = t // NY, t % NY
            out.append(
                jnp.concatenate([panel[i, (2 * k + h) * NY + yy] for h in range(2)], axis=0)
            )
        return jnp.concatenate(out, axis=1)

    def keep_gram(cp, d, gram):
        packed = jnp.concatenate([gram[8 * j : 8 * j + 8, :] for j in range(R // 8)], axis=1)
        kbuf[cp, d, me_t] = packed

    def send_gram(cp, d):
        mine = kbuf.at[cp, d, me_t]
        for o in (1, 2, 3, 4, 5, 6, 7):
            send(mine, mine, ks_sem.at[cp], kr_sem.at[cp, d], dev_t((me_t + o) % NT))

    def send_sums(cp, d):
        mine = ux.at[cp, d, me_t]
        for o in (4, 3, 5, 2, 6, 1, 7):
            send(mine, mine, uxs_sem.at[cp], uxr_sem.at[cp, d], dev_t((me_t + o) % NT))

    def last_tensor(cp):
        settle(kbuf.at[cp, 0, pl.ds(0, NT - 1)], ks_sem.at[cp])
        settle(ux.at[cp, 0, pl.ds(0, NT - 1)], uxs_sem.at[cp])

    def last_wide(w):
        settle(ysend.at[w, 0, pl.ds(0, NZ * (NY - 1)), pl.ds(0, span)], ys_sem.at[w])
        settle(ysend.at[w, 0, pl.ds(0, 2 * (GROUPS - 1)), last_part], ysx_sem.at[w])
        settle(zsend.at[w, 0, pl.ds(0, NZ - 1), pl.ds(0, span)], zs_sem.at[w])
        settle(up_wide.at[0, pl.ds(0, SLOTS - 1), pl.ds(0, span)], ag_sem.at[w])
        settle(up_wide.at[0, pl.ds(0, 2 * (NY - 1)), last_part], agx_sem.at[w])
        for h in range(2):

            @pl.when(z != 2 * y + h)
            def _():
                settle(zsend.at[w, 0, h, last_part], zsx_sem.at[w, h])

        @pl.when(z // 2 == y)
        def _():
            settle(up_wide.at[0, pl.ds(0, NZ - 1), last_part], agzs_sem.at[w])

    def last_narrow(w):
        settle(nsend.at[w, 0, pl.ds(0, SLOTS - 1)], ns_sem.at[w])
        settle(up_narrow.at[0, pl.ds(0, SLOTS - 1)], nag_sem.at[w])

    def wait_wide(w, kk):
        settle(up_wide.at[0, pl.ds(0, 2 * (NY - 1)), pl.ds(0, span)], agy_sem.at[w, kk])

        @pl.when(kk != y)
        def _():
            settle(up_wide.at[0, pl.ds(0, 2), last_part], agyx_sem.at[w, kk])

    def wait_narrow(w):
        settle(up_narrow.at[0, pl.ds(0, SLOTS - 1)], nagr_sem.at[w])

    def sums_wide(cp, d, panel, w, rows, start=False):
        total = jnp.zeros((R, tokens), jnp.float32)
        for n, o in enumerate((0, 1, 3, 2)):
            kk = (z // 2 + o) % GROUPS
            if not start:
                wait_wide(w, kk)
            part = wide_group(panel, d, kk)
            kparts[kk] = nt_dot(part, part)
            if n == GROUPS - 1:
                keep_gram(cp, d, ((kparts[0] + kparts[1]) + kparts[2]) + kparts[3])
                if not start:
                    send_gram(cp, d)
            at = pl.ds(pl.multiple_of(kk * cols, LANES), cols)
            total = total + nt_dot(part, rows[:, at])
        ux[cp, d, me_t] = total.astype(jnp.bfloat16)
        if not start:
            send_sums(cp, d)

    def sums_narrow(cp, d, panel, w, rows, start=False):
        if not start:
            wait_narrow(w)
        part = narrow_all(panel, d)
        keep_gram(cp, d, nt_dot(part, part))
        if not start:
            send_gram(cp, d)
        ux[cp, d, me_t] = nt_dot(part, rows[...]).astype(jnp.bfloat16)
        if not start:
            send_sums(cp, d)

    def tokens_done(cp, d, first):
        settle(kbuf.at[cp, d, pl.ds(0, NT - 1)], kr_sem.at[cp, d])
        packed = kbuf[cp, d, 0]
        for t in range(1, NT):
            packed = packed + kbuf[cp, d, t]
        gram = jnp.concatenate([packed[:, R * j : R * j + R] for j in range(R // 8)], axis=0)
        inverse = invert_factor(gram)
        if first:
            row = lax.broadcasted_iota(jnp.int32, (R, R), 0)
            col = lax.broadcasted_iota(jnp.int32, (R, R), 1)
            identity = jnp.where(row == col, 1.0, 0.0)
            inverse = jnp.where(jnp.full((R, R), d) == 0, identity, inverse)
        settle(ux.at[cp, d, pl.ds(0, NT - 1)], uxr_sem.at[cp, d])
        total = ux[cp, d, 0].astype(jnp.float32)
        for t in range(1, NT):
            total = total + ux[cp, d, t].astype(jnp.float32)
        return inverse, nn_dot(inverse, total, lax.Precision.HIGHEST).astype(jnp.bfloat16)

    def scatter_wide(w, d, tok, rows):
        @pl.when(d > 0)
        def _():
            last_wide(w)

        for o in (2, 1, 3, 0):
            kk = (z // 2 + o) % GROUPS
            at = pl.ds(pl.multiple_of(kk * cols, LANES), cols)
            part = nn_dot(tok, rows[:, at]).astype(jnp.bfloat16)
            for h in range(2):
                for yy in range(NY):
                    for i in range(span + 1):
                        lo = (yy * span + i) * LANES
                        ysend[w, d, (2 * kk + h) * NY + yy, i] = part[
                            HALF * h : HALF * h + HALF, lo : lo + LANES
                        ]
            for h in range(2):
                zd = 2 * kk + h
                for q in (2, 1, 3):
                    yd = (y + q) % NY
                    part = core_part(yd, kk)
                    send(
                        ysend.at[w, d, zd * NY + yd, part], yrecv.at[w, d, zd, q - 1, part],
                        ys_sem.at[w], yr_sem.at[w, zd], dev_dp(z, yd),
                    )

            @pl.when(kk != y)
            def _():
                for h in range(2):
                    zd = 2 * kk + h
                    q = (kk + NY - y) % NY
                    send(
                        ysend.at[w, d, zd * NY + kk, last_part],
                        yrecv.at[w, d, zd, q - 1, last_part],
                        ysx_sem.at[w], yx_sem.at[w, h], dev_dp(z, kk),
                    )

    def reduce_wide(w, d):
        for o in FAR + (0,):
            zd = (z + o) % NZ
            settle(yrecv.at[w, d, zd, pl.ds(0, NY - 1), pl.ds(0, span)], yr_sem.at[w, zd])

            @pl.when(zd // 2 == y)
            def _():
                settle(yrecv.at[w, d, zd, pl.ds(0, NY - 1), last_part], yx_sem.at[w, zd % 2])

            total = ysend[w, d, zd * NY + y].astype(jnp.float32)
            for q in range(NY - 1):
                total = total + yrecv[w, d, zd, q].astype(jnp.float32)
            if o:
                zsend[w, d, zd] = total.astype(jnp.bfloat16)
                part = core_part(y, zd // 2)
                send(
                    zsend.at[w, d, zd, part], zrecv.at[w, d, o - 1, part],
                    zs_sem.at[w], zr_sem.at[w], dev_dp(zd, y),
                )

                @pl.when(zd // 2 == y)
                def _():
                    send(
                        zsend.at[w, d, zd, last_part], zrecv.at[w, d, o - 1, last_part],
                        zsx_sem.at[w, zd % 2], zx_sem.at[w], dev_dp(zd, y),
                    )

            else:
                zown[w] = total

    def to_y(w, panel, i, zs):
        s = zs * NY + y
        piece = panel.at[i, s, core_part(y, zs // 2)]
        for q in (2, 1, 3):
            send(piece, piece, ag_sem.at[w], agy_sem.at[w, zs // 2], dev_dp(z, (y + q) % NY))

        @pl.when(zs // 2 == y)
        def _():
            last = panel.at[i, s, last_part]
            for q in (2, 1, 3):
                send(last, last, agx_sem.at[w], agyx_sem.at[w, zs // 2], dev_dp(z, (y + q) % NY))

    def gather_wide(w, d, panel, i):
        settle(zrecv.at[w, d, pl.ds(0, NZ - 1), pl.ds(0, span)], zr_sem.at[w])

        @pl.when(z // 2 == y)
        def _():
            settle(zrecv.at[w, d, pl.ds(0, NZ - 1), last_part], zx_sem.at[w])

        total = zown[w]
        for q in range(NZ - 1):
            total = total + zrecv[w, d, q].astype(jnp.float32)
        panel[i, slot] = total.astype(jnp.bfloat16)
        piece = panel.at[i, slot, core_part(y, z // 2)]
        for o in NEAR:
            send(piece, piece, ag_sem.at[w], agz_sem.at[w, o - 1], dev_dp((z + o) % NZ, y))

        @pl.when(z // 2 == y)
        def _():
            last = panel.at[i, slot, last_part]
            for o in NEAR:
                send(last, last, agzs_sem.at[w], agzx_sem.at[w, o - 1], dev_dp((z + o) % NZ, y))

        to_y(w, panel, i, z)

    def forward_wide(w, panel, i):
        for o in NEAR:
            zs = (z + NZ - o) % NZ
            settle(panel.at[i, zs * NY + y, pl.ds(0, span)], agz_sem.at[w, o - 1])

            @pl.when(zs // 2 == y)
            def _():
                settle(panel.at[i, zs * NY + y, last_part], agzx_sem.at[w, o - 1])

            to_y(w, panel, i, zs)

    def direct(src, dst, send_sem, recv_sem):
        for o in FAR + (0,):
            for q in (2, 1, 3, 0):
                if o or q:
                    zd, yd = (z + o) % NZ, (y + q) % NY
                    send(src(zd * NY + yd), dst, send_sem, recv_sem, dev_dp(zd, yd))

    def scatter_narrow(w, d, tok, rows):
        @pl.when(d > 0)
        def _():
            last_narrow(w)

        part = nn_dot(tok, rows[...]).astype(jnp.bfloat16)
        for t in range(SLOTS // 2):
            k, yy = t // NY, t % NY
            for h in range(2):
                nsend[w, d, (2 * k + h) * NY + yy] = part[
                    HALF * h : HALF * h + HALF, t * LANES : (t + 1) * LANES
                ]
        direct(lambda s: nsend.at[w, d, s], nrecv.at[w, d, slot], ns_sem.at[w], nr_sem.at[w])

    def gather_narrow(w, d, panel, i):
        settle(nrecv.at[w, d, pl.ds(0, SLOTS - 1)], nr_sem.at[w])
        nrecv[w, d, slot] = nsend[w, d, slot]
        total = nrecv[w, d, 0].astype(jnp.float32)
        for s in range(1, SLOTS):
            total = total + nrecv[w, d, s].astype(jnp.float32)
        panel[i, slot] = total.astype(jnp.bfloat16)
        piece = panel.at[i, slot]
        direct(lambda s: piece, piece, nag_sem.at[w], nagr_sem.at[w])

    def orthonormal(inverse, part):
        return nn_dot(inverse, part.astype(jnp.float32), lax.Precision.HIGHEST).astype(jnp.bfloat16)

    def pair(d, _):
        @pl.when(d == 0)
        def _():
            loads[4].wait()
            loads[5].wait()

        _, tok = tokens_done(2, d, True)
        scatter_wide(1, d, tok, h_v)
        _, tok = tokens_done(0, d, True)
        scatter_narrow(0, d, tok, x_v)
        reduce_wide(1, d)
        gather_narrow(0, d, up_narrow, d)
        gather_wide(1, d, dn_wide, d)
        forward_wide(1, dn_wide, d)

        @pl.when(d > 0)
        def _():
            last_tensor(1)
            last_tensor(3)

        sums_narrow(1, d, up_narrow, 0, x_v)
        sums_wide(3, d, dn_wide, 1, h_v)
        inverse, tok = tokens_done(1, d, False)
        scatter_wide(0, d, tok, gu_v)

        @pl.when(d == PAIRS - 1)
        def _():
            qn_v[...] = orthonormal(inverse, narrow_all(up_narrow, d))
            pltpu.make_async_copy(qn_v, up_q, out_sem.at[0]).start()

        inverse, tok = tokens_done(3, d, False)
        scatter_narrow(1, d, tok, gd_v)

        @pl.when(d == PAIRS - 1)
        def _():
            for k in range(GROUPS):
                qw_v[:, k * cols : (k + 1) * cols] = orthonormal(inverse, wide_group(dn_wide, d, k))
            pltpu.make_async_copy(qw_v, down_q, out_sem.at[1]).start()

        reduce_wide(0, d)
        gather_wide(0, d, up_wide, d + 1)
        gather_narrow(1, d, dn_narrow, d + 1)
        forward_wide(0, up_wide, d + 1)

        @pl.when(d + 1 < PAIRS)
        def _():
            last_tensor(2)
            last_tensor(0)
            sums_narrow(2, d + 1, dn_narrow, 1, gd_v)
            sums_wide(0, d + 1, up_wide, 0, gu_v)

        return 0

    sums_narrow(2, 0, dn_narrow, 1, gd_v, True)
    sums_wide(0, 0, up_wide, 0, gu_v, True)
    pl.semaphore_wait(barrier, len(peers))
    for cp in (2, 0):
        send_gram(cp, 0)
        send_sums(cp, 0)
    lax.fori_loop(0, PAIRS, pair, 0)

    wait_narrow(1)
    down_out = pltpu.make_async_copy(dn_narrow.at[PAIRS], down_img, out_sem.at[2])
    down_out.start()
    for k in range(GROUPS):
        wait_wide(0, k)
    up_out = pltpu.make_async_copy(up_wide.at[PAIRS], up_img, out_sem.at[3])
    up_out.start()
    for cp in range(4):
        last_tensor(cp)
    for w in range(2):
        last_wide(w)
        last_narrow(w)
    pltpu.make_async_copy(qn_v, up_q, out_sem.at[0]).wait()
    pltpu.make_async_copy(qw_v, down_q, out_sem.at[1]).wait()
    down_out.wait()
    up_out.wait()


def finish(scales, up_q, up_img, down_q, down_img, up_a, up_b, down_a, down_b, uq, ui, dq, di, ua, ub, da, db, sem):
    up_scale, down_scale, scale = scales
    loads = [
        pltpu.make_async_copy(src, dst, sem.at[i])
        for i, (src, dst) in enumerate(((up_q, uq), (down_q, dq), (down_img, di), (up_img, ui)))
    ]
    for load in loads:
        load.start()
    stores = [
        pltpu.make_async_copy(src, dst, sem.at[4 + i])
        for i, (src, dst) in enumerate(((ua, up_a), (da, down_a), (db, down_b), (ub, up_b)))
    ]
    loads[0].wait()
    ua[...] = uq[...].astype(jnp.float32) * up_scale
    stores[0].start()
    loads[1].wait()
    da[...] = dq[...].astype(jnp.float32) * down_scale
    stores[1].start()
    tiles = ub.shape[1] // LANES // GROUPS
    span = tiles // NY
    loads[2].wait()
    for k in range(GROUPS):
        for h in range(2):
            for yy in range(NY):
                lo = (k * NY + yy) * LANES
                piece = di[(2 * k + h) * NY + yy]
                db[HALF * h : HALF * h + HALF, lo : lo + LANES] = piece.astype(jnp.float32) * scale
    stores[2].start()
    loads[3].wait()
    for k in range(GROUPS):
        for h in range(2):
            for t in range(tiles):
                yy, n = place(t, span, k)
                lo = (k * tiles + t) * LANES
                piece = ui[(2 * k + h) * NY + yy, n]
                ub[HALF * h : HALF * h + HALF, lo : lo + LANES] = piece.astype(jnp.float32) * scale
    stores[3].start()
    for store in stores:
        store.wait()


def local(x_in, grad_up, hidden_act, grad_down, sketch_up, sketch_down):
    tokens, n_narrow = x_in.shape
    n_wide = grad_up.shape[1]
    tail = (HALF, LANES)
    piece = (n_wide // LANES // GROUPS // NY + 1,) + tail
    bf16, f32 = jnp.bfloat16, jnp.float32
    dma = pltpu.SemaphoreType.DMA
    vmem = pltpu.VMEM
    scratch = [
        vmem((tokens, n_narrow), bf16),
        vmem((tokens, n_wide), bf16),
        vmem((tokens, n_wide), bf16),
        vmem((tokens, n_narrow), bf16),
        vmem((R, n_wide), bf16),
        vmem((R, n_narrow), bf16),
        vmem((R, n_narrow), bf16),
        vmem((R, n_wide), bf16),
        vmem((PAIRS + 1, SLOTS) + piece, bf16),
        vmem((PAIRS, SLOTS) + tail, bf16),
        vmem((PAIRS, SLOTS) + piece, bf16),
        vmem((PAIRS + 1, SLOTS) + tail, bf16),
        vmem((2, PAIRS, SLOTS) + piece, bf16),
        vmem((2, PAIRS, NZ, NY - 1) + piece, bf16),
        vmem((2,) + piece, f32),
        vmem((2, PAIRS, NZ) + piece, bf16),
        vmem((2, PAIRS, NZ - 1) + piece, bf16),
        vmem((2, PAIRS, SLOTS) + tail, bf16),
        vmem((2, PAIRS, SLOTS) + tail, bf16),
        vmem((4, PAIRS, NT, R, tokens), bf16),
        vmem((GROUPS, R, R), f32),
        vmem((4, PAIRS, NT, 8, LANES), f32),
        dma((6,)), dma((4,)), dma((2,)), dma((2, NZ)), dma((2,)), dma((2,)),
        dma((2,)), dma((2, NZ - 1)), dma((2, GROUPS)),
        dma((2,)), dma((2,)), dma((2,)), dma((2,)),
        dma((4,)), dma((4, PAIRS)), dma((4,)), dma((4, PAIRS)),
        dma((2,)), dma((2, 2)), dma((2, 2)), dma((2,)),
        dma((2,)), dma((2,)), dma((2, NZ - 1)), dma((2, GROUPS)),
    ]
    panels = pl.pallas_call(
        kernel,
        out_shape=(
            jax.ShapeDtypeStruct((R, n_narrow), bf16),
            jax.ShapeDtypeStruct((SLOTS,) + piece, bf16),
            jax.ShapeDtypeStruct((R, n_wide), bf16),
            jax.ShapeDtypeStruct((SLOTS,) + tail, bf16),
        ),
        in_specs=[pl.BlockSpec(memory_space=pl.ANY)] * 6,
        out_specs=[pl.BlockSpec(memory_space=pl.ANY)] * 4,
        scratch_shapes=scratch,
        compiler_params=pltpu.CompilerParams(
            collective_id=0, has_side_effects=True, vmem_limit_bytes=56 * 2**20
        ),
    )(x_in, grad_up, hidden_act, grad_down, sketch_up, sketch_down)
    width = lax.axis_size("tensor")
    scales = (
        math.sqrt(n_narrow * width),
        math.sqrt(n_wide * width),
        1.0 / math.sqrt(tokens * lax.axis_size("dp")),
    )
    outs = (
        jax.ShapeDtypeStruct((R, n_narrow), f32),
        jax.ShapeDtypeStruct((R, n_wide), f32),
        jax.ShapeDtypeStruct((R, n_wide), f32),
        jax.ShapeDtypeStruct((R, n_narrow), f32),
    )
    return pl.pallas_call(
        functools.partial(finish, scales),
        out_shape=outs,
        in_specs=[pl.BlockSpec(memory_space=pl.ANY)] * 4,
        out_specs=[pl.BlockSpec(memory_space=pl.ANY)] * 4,
        scratch_shapes=[vmem(a.shape, a.dtype) for a in tuple(panels) + outs] + [dma((8,))],
        compiler_params=pltpu.CompilerParams(vmem_limit_bytes=56 * 2**20),
    )(*panels)


def solution(mesh):
    in_specs = (
        P("dp", "tensor"),
        P("dp", "tensor"),
        P("dp", "tensor"),
        P("dp", "tensor"),
        P(None, "tensor"),
        P(None, "tensor"),
    )
    out_specs = (P(None, "tensor"), P(None, "tensor"), P(None, "tensor"), P(None, "tensor"))
    return jax.shard_map(local, mesh=mesh, in_specs=in_specs, out_specs=out_specs, check_vma=False)
```

```python
import functools
import math

import jax
import jax.numpy as jnp
from jax import lax
from jax.experimental import pallas as pl
from jax.experimental.pallas import tpu as pltpu
from jax.sharding import PartitionSpec as P

MESH = pl.DeviceIdType.MESH

NZ, NY, NX, NC = 8, 4, 4, 2
R = 32
ITERS = 2
PAIRS = ITERS + 1
HALF = R // 2
LANES = 128
GROUPS = NZ // 2
SLOTS = NZ * NY
NT = NX * NC
BLOCK = 16

FAR = (4, 3, 5, 2, 6, 1, 7)
NEAR = (1, 7, 2, 6, 3, 5, 4)


def nt_dot(a, b):
    return lax.dot_general(a, b, (((1,), (1,)), ((), ())), preferred_element_type=jnp.float32)


def nn_dot(a, b, precision=None):
    return lax.dot_general(
        a, b, (((1,), (0,)), ((), ())), precision=precision, preferred_element_type=jnp.float32
    )


def invert_factor(gram):
    lane = lax.broadcasted_iota(jnp.int32, (R, LANES), 1)
    row = lax.broadcasted_iota(jnp.int32, (R, LANES), 0)
    right = lane >= R
    padded = jnp.concatenate([gram, jnp.zeros((R, LANES - R), jnp.float32)], axis=1)
    work = jnp.where(right, jnp.where(lane - R == row, 1.0, 0.0), padded)
    scale = jnp.zeros((R, LANES), jnp.float32)
    for b in range(0, R, BLOCK):
        cols = [jnp.broadcast_to(work[:, b + j : b + j + 1], (R, LANES)) for j in range(BLOCK)]
        for j in range(BLOCK):
            k = b + j
            pivot = jnp.broadcast_to(cols[j][k : k + 1, :], (R, LANES))
            scale = jnp.where(row == k, lax.rsqrt(pivot), scale)
            factor = jnp.where(row > k, cols[j] * (1.0 / pivot), 0.0)
            for i in range(j + 1, BLOCK):
                cols[i] = cols[i] - factor * jnp.broadcast_to(cols[i][k : k + 1, :], (R, LANES))
            work = work - factor * jnp.broadcast_to(work[k : k + 1, :], (R, LANES))
    return (work * scale)[:, R : 2 * R]


def place(t, span, k):
    row = min(t // span, NY - 1)
    if t % span or row == 0 or t // span > row:
        return row, t - span * row
    if isinstance(k, int):
        return (row - 1, span) if row > k else (row, 0)
    return jnp.where(row > k, row - 1, row), jnp.where(row > k, span, 0)


def settle(ref, sem):
    pltpu.make_async_copy(ref, ref, sem).wait()


def kernel(
    x_in, grad_up, hidden_act, grad_down, sketch_up, sketch_down,
    up_q, up_img, down_q, down_img,
    x_v, gu_v, h_v, gd_v, sk_wide, sk_narrow, qn_v, qw_v,
    up_wide, up_narrow, dn_wide, dn_narrow,
    ysend, yrecv, zown, zsend, zrecv, nsend, nrecv,
    ux, kparts, kbuf,
    in_sem, out_sem, ys_sem, yr_sem, zs_sem, zr_sem, ag_sem, agz_sem, agy_sem,
    ns_sem, nr_sem, nag_sem, nagr_sem, ks_sem, kr_sem, uxs_sem, uxr_sem,
    ysx_sem, yx_sem, zsx_sem, zx_sem, agx_sem, agzs_sem, agzx_sem, agyx_sem,
):
    dp = lax.axis_index("dp")
    me_t = lax.axis_index("tensor")
    z, y = dp // NY, dp % NY
    x, c = me_t // NC, me_t % NC
    slot = dp
    n_wide, n_narrow = gu_v.shape[1], x_v.shape[1]
    tiles = n_wide // LANES // GROUPS
    span = tiles // NY
    cols = tiles * LANES
    tokens = gu_v.shape[0]

    loads = [
        pltpu.make_async_copy(src, dst, in_sem.at[i])
        for i, (src, dst) in enumerate(
            (
                (sketch_down, sk_narrow),
                (sketch_up, sk_wide),
                (grad_down, gd_v),
                (grad_up, gu_v),
                (hidden_act, h_v),
                (x_in, x_v),
            )
        )
    ]
    for load in loads:
        load.start()

    def dev_dp(zz, yy):
        return (zz * NY + yy, me_t)

    def dev_t(tt):
        return (dp, tt)

    def send(src, dst, send_sem, recv_sem, device):
        pltpu.make_async_remote_copy(
            src, dst, send_sem, recv_sem, device_id=device, device_id_type=MESH
        ).start()

    barrier = pltpu.get_barrier_semaphore()
    peers = [((dp + o) % SLOTS, me_t) for o in range(1, SLOTS)]
    peers += [dev_t((me_t + o) % NT) for o in range(1, NT)]
    for peer in peers:
        pl.semaphore_signal(barrier, inc=1, device_id=peer, device_id_type=MESH)

    for load in loads[:4]:
        load.wait()

    for k in range(GROUPS):
        for h in range(2):
            rows = slice(HALF * h, HALF * h + HALF)
            for yy in range(NY):
                s = (2 * k + h) * NY + yy
                for i in range(span + 1):
                    lo = (k * tiles + yy * span + i) * LANES
                    up_wide[0, s, i] = sk_wide[rows, lo : lo + LANES]
                lo = (k * NY + yy) * LANES
                dn_narrow[0, s] = sk_narrow[rows, lo : lo + LANES]

    def core_part(yy, kk):
        return pl.ds(jnp.where(yy > kk, 1, 0), span)

    last_part = pl.ds(span, 1)

    def wide_group(panel, i, kk):
        out = []
        for t in range(tiles):
            yy, n = place(t, span, kk)
            out.append(
                jnp.concatenate([panel[i, (2 * kk + h) * NY + yy, n] for h in range(2)], axis=0)
            )
        return jnp.concatenate(out, axis=1)

    def narrow_all(panel, i):
        out = []
        for t in range(SLOTS // 2):
            k, yy = t // NY, t % NY
            out.append(
                jnp.concatenate([panel[i, (2 * k + h) * NY + yy] for h in range(2)], axis=0)
            )
        return jnp.concatenate(out, axis=1)

    def keep_gram(cp, d, gram):
        packed = jnp.concatenate([gram[8 * j : 8 * j + 8, :] for j in range(R // 8)], axis=1)
        kbuf[cp, d, me_t] = packed

    def send_gram(cp, d):
        mine = kbuf.at[cp, d, me_t]
        for o in (1, 2, 3, 4, 5, 6, 7):
            send(mine, mine, ks_sem.at[cp], kr_sem.at[cp, d], dev_t((me_t + o) % NT))

    def send_sums(cp, d):
        mine = ux.at[cp, d, me_t]
        for o in (4, 3, 5, 2, 6, 1, 7):
            send(mine, mine, uxs_sem.at[cp], uxr_sem.at[cp, d], dev_t((me_t + o) % NT))

    def last_tensor(cp):
        settle_gram(cp)
        settle_sums(cp)

    def settle_gram(cp):
        settle(kbuf.at[cp, 0, pl.ds(0, NT - 1)], ks_sem.at[cp])

    def settle_sums(cp):
        settle(ux.at[cp, 0, pl.ds(0, NT - 1)], uxs_sem.at[cp])

    def last_wide(w):
        settle(ysend.at[w, 0, pl.ds(0, NZ * (NY - 1)), pl.ds(0, span)], ys_sem.at[w])
        settle(ysend.at[w, 0, pl.ds(0, 2 * (GROUPS - 1)), last_part], ysx_sem.at[w])
        settle(zsend.at[w, 0, pl.ds(0, NZ - 1), pl.ds(0, span)], zs_sem.at[w])
        settle(up_wide.at[0, pl.ds(0, SLOTS - 1), pl.ds(0, span)], ag_sem.at[w])
        settle(up_wide.at[0, pl.ds(0, 2 * (NY - 1)), last_part], agx_sem.at[w])
        for h in range(2):

            @pl.when(z != 2 * y + h)
            def _():
                settle(zsend.at[w, 0, h, last_part], zsx_sem.at[w, h])

        @pl.when(z // 2 == y)
        def _():
            settle(up_wide.at[0, pl.ds(0, NZ - 1), last_part], agzs_sem.at[w])

    def last_narrow(w):
        settle(nsend.at[w, 0, pl.ds(0, SLOTS - 1)], ns_sem.at[w])
        settle(up_narrow.at[0, pl.ds(0, SLOTS - 1)], nag_sem.at[w])

    def wait_wide(w, kk):
        settle(up_wide.at[0, pl.ds(0, 2 * (NY - 1)), pl.ds(0, span)], agy_sem.at[w, kk])

        @pl.when(kk != y)
        def _():
            settle(up_wide.at[0, pl.ds(0, 2), last_part], agyx_sem.at[w, kk])

    def wait_narrow(w):
        settle(up_narrow.at[0, pl.ds(0, SLOTS - 1)], nagr_sem.at[w])

    def sums_wide(cp, d, panel, w, rows, start=False):
        total = jnp.zeros((R, tokens), jnp.float32)
        for n, o in enumerate((0, 1, 3, 2)):
            kk = (z // 2 + o) % GROUPS
            if not start:
                wait_wide(w, kk)
            part = wide_group(panel, d, kk)
            if not start:
                kparts[kk] = nt_dot(part, part)
                if n == GROUPS - 1:
                    keep_gram(cp, d, ((kparts[0] + kparts[1]) + kparts[2]) + kparts[3])
                    send_gram(cp, d)
            at = pl.ds(pl.multiple_of(kk * cols, LANES), cols)
            total = total + nt_dot(part, rows[:, at])
        ux[cp, d, me_t] = total.astype(jnp.bfloat16)
        if not start:
            send_sums(cp, d)

    def sums_narrow(cp, d, panel, w, rows, start=False):
        if not start:
            wait_narrow(w)
        part = narrow_all(panel, d)
        if not start:
            keep_gram(cp, d, nt_dot(part, part))
            send_gram(cp, d)
        ux[cp, d, me_t] = nt_dot(part, rows[...]).astype(jnp.bfloat16)
        if not start:
            send_sums(cp, d)

    def tokens_done(cp, d, first):
        @pl.when(d > 0 if first else d >= 0)
        def _():
            settle(kbuf.at[cp, d, pl.ds(0, NT - 1)], kr_sem.at[cp, d])

        packed = kbuf[cp, d, 0]
        for t in range(1, NT):
            packed = packed + kbuf[cp, d, t]
        gram = jnp.concatenate([packed[:, R * j : R * j + R] for j in range(R // 8)], axis=0)
        inverse = invert_factor(gram)
        if first:
            row = lax.broadcasted_iota(jnp.int32, (R, R), 0)
            col = lax.broadcasted_iota(jnp.int32, (R, R), 1)
            identity = jnp.where(row == col, 1.0, 0.0)
            inverse = jnp.where(jnp.full((R, R), d) == 0, identity, inverse)
        settle(ux.at[cp, d, pl.ds(0, NT - 1)], uxr_sem.at[cp, d])
        total = ux[cp, d, 0].astype(jnp.float32)
        for t in range(1, NT):
            total = total + ux[cp, d, t].astype(jnp.float32)
        return inverse, nn_dot(inverse, total, lax.Precision.HIGHEST).astype(jnp.bfloat16)

    def scatter_wide(w, d, tok, rows):
        @pl.when(d > 0)
        def _():
            last_wide(w)

        for o in (2, 1, 3, 0):
            kk = (z // 2 + o) % GROUPS
            at = pl.ds(pl.multiple_of(kk * cols, LANES), cols)
            part = nn_dot(tok, rows[:, at]).astype(jnp.bfloat16)
            for h in range(2):
                for yy in range(NY):
                    for i in range(span + 1):
                        lo = (yy * span + i) * LANES
                        ysend[w, d, (2 * kk + h) * NY + yy, i] = part[
                            HALF * h : HALF * h + HALF, lo : lo + LANES
                        ]
            for h in range(2):
                zd = 2 * kk + h
                for q in (2, 1, 3):
                    yd = (y + q) % NY
                    part = core_part(yd, kk)
                    send(
                        ysend.at[w, d, zd * NY + yd, part], yrecv.at[w, d, zd, q - 1, part],
                        ys_sem.at[w], yr_sem.at[w, zd], dev_dp(z, yd),
                    )

            @pl.when(kk != y)
            def _():
                for h in range(2):
                    zd = 2 * kk + h
                    q = (kk + NY - y) % NY
                    send(
                        ysend.at[w, d, zd * NY + kk, last_part],
                        yrecv.at[w, d, zd, q - 1, last_part],
                        ysx_sem.at[w], yx_sem.at[w, h], dev_dp(z, kk),
                    )

    def reduce_wide(w, d):
        for o in FAR + (0,):
            zd = (z + o) % NZ
            settle(yrecv.at[w, d, zd, pl.ds(0, NY - 1), pl.ds(0, span)], yr_sem.at[w, zd])

            @pl.when(zd // 2 == y)
            def _():
                settle(yrecv.at[w, d, zd, pl.ds(0, NY - 1), last_part], yx_sem.at[w, zd % 2])

            total = ysend[w, d, zd * NY + y].astype(jnp.float32)
            for q in range(NY - 1):
                total = total + yrecv[w, d, zd, q].astype(jnp.float32)
            if o:
                zsend[w, d, zd] = total.astype(jnp.bfloat16)
                part = core_part(y, zd // 2)
                send(
                    zsend.at[w, d, zd, part], zrecv.at[w, d, o - 1, part],
                    zs_sem.at[w], zr_sem.at[w], dev_dp(zd, y),
                )

                @pl.when(zd // 2 == y)
                def _():
                    send(
                        zsend.at[w, d, zd, last_part], zrecv.at[w, d, o - 1, last_part],
                        zsx_sem.at[w, zd % 2], zx_sem.at[w], dev_dp(zd, y),
                    )

            else:
                zown[w] = total

    def to_y(w, panel, i, zs):
        s = zs * NY + y
        piece = panel.at[i, s, core_part(y, zs // 2)]
        for q in (2, 1, 3):
            send(piece, piece, ag_sem.at[w], agy_sem.at[w, zs // 2], dev_dp(z, (y + q) % NY))

        @pl.when(zs // 2 == y)
        def _():
            last = panel.at[i, s, last_part]
            for q in (2, 1, 3):
                send(last, last, agx_sem.at[w], agyx_sem.at[w, zs // 2], dev_dp(z, (y + q) % NY))

    def gather_wide(w, d, panel, i):
        settle(zrecv.at[w, d, pl.ds(0, NZ - 1), pl.ds(0, span)], zr_sem.at[w])

        @pl.when(z // 2 == y)
        def _():
            settle(zrecv.at[w, d, pl.ds(0, NZ - 1), last_part], zx_sem.at[w])

        total = zown[w]
        for q in range(NZ - 1):
            total = total + zrecv[w, d, q].astype(jnp.float32)
        panel[i, slot] = total.astype(jnp.bfloat16)
        piece = panel.at[i, slot, core_part(y, z // 2)]
        for o in NEAR:
            send(piece, piece, ag_sem.at[w], agz_sem.at[w, o - 1], dev_dp((z + o) % NZ, y))

        @pl.when(z // 2 == y)
        def _():
            last = panel.at[i, slot, last_part]
            for o in NEAR:
                send(last, last, agzs_sem.at[w], agzx_sem.at[w, o - 1], dev_dp((z + o) % NZ, y))

        to_y(w, panel, i, z)

    def forward_wide(w, panel, i):
        for o in NEAR:
            zs = (z + NZ - o) % NZ
            settle(panel.at[i, zs * NY + y, pl.ds(0, span)], agz_sem.at[w, o - 1])

            @pl.when(zs // 2 == y)
            def _():
                settle(panel.at[i, zs * NY + y, last_part], agzx_sem.at[w, o - 1])

            to_y(w, panel, i, zs)

    def direct(src, dst, send_sem, recv_sem):
        for o in FAR + (0,):
            for q in (2, 1, 3, 0):
                if o or q:
                    zd, yd = (z + o) % NZ, (y + q) % NY
                    send(src(zd * NY + yd), dst, send_sem, recv_sem, dev_dp(zd, yd))

    def scatter_narrow(w, d, tok, rows):
        @pl.when(d > 0)
        def _():
            last_narrow(w)

        part = nn_dot(tok, rows[...]).astype(jnp.bfloat16)
        for t in range(SLOTS // 2):
            k, yy = t // NY, t % NY
            for h in range(2):
                nsend[w, d, (2 * k + h) * NY + yy] = part[
                    HALF * h : HALF * h + HALF, t * LANES : (t + 1) * LANES
                ]
        direct(lambda s: nsend.at[w, d, s], nrecv.at[w, d, slot], ns_sem.at[w], nr_sem.at[w])

    def gather_narrow(w, d, panel, i):
        settle(nrecv.at[w, d, pl.ds(0, SLOTS - 1)], nr_sem.at[w])
        nrecv[w, d, slot] = nsend[w, d, slot]
        total = nrecv[w, d, 0].astype(jnp.float32)
        for s in range(1, SLOTS):
            total = total + nrecv[w, d, s].astype(jnp.float32)
        panel[i, slot] = total.astype(jnp.bfloat16)
        piece = panel.at[i, slot]
        direct(lambda s: piece, piece, nag_sem.at[w], nagr_sem.at[w])

    def orthonormal(inverse, part):
        return nn_dot(inverse, part.astype(jnp.float32), lax.Precision.HIGHEST).astype(jnp.bfloat16)

    def pair(d, _):
        @pl.when(d == 0)
        def _():
            loads[4].wait()
            loads[5].wait()

        _, tok = tokens_done(2, d, True)
        scatter_wide(1, d, tok, h_v)
        _, tok = tokens_done(0, d, True)
        scatter_narrow(0, d, tok, x_v)
        reduce_wide(1, d)
        gather_narrow(0, d, up_narrow, d)
        gather_wide(1, d, dn_wide, d)
        forward_wide(1, dn_wide, d)

        @pl.when(d > 0)
        def _():
            last_tensor(1)
            last_tensor(3)

        sums_narrow(1, d, up_narrow, 0, x_v)
        sums_wide(3, d, dn_wide, 1, h_v)
        inverse, tok = tokens_done(1, d, False)
        scatter_wide(0, d, tok, gu_v)

        @pl.when(d == PAIRS - 1)
        def _():
            qn_v[...] = orthonormal(inverse, narrow_all(up_narrow, d))
            pltpu.make_async_copy(qn_v, up_q, out_sem.at[0]).start()

        inverse, tok = tokens_done(3, d, False)
        scatter_narrow(1, d, tok, gd_v)

        @pl.when(d == PAIRS - 1)
        def _():
            for k in range(GROUPS):
                qw_v[:, k * cols : (k + 1) * cols] = orthonormal(inverse, wide_group(dn_wide, d, k))
            pltpu.make_async_copy(qw_v, down_q, out_sem.at[1]).start()

        reduce_wide(0, d)
        gather_wide(0, d, up_wide, d + 1)
        gather_narrow(1, d, dn_narrow, d + 1)
        forward_wide(0, up_wide, d + 1)

        @pl.when(d + 1 < PAIRS)
        def _():
            for cp in (2, 0):
                settle_sums(cp)

                @pl.when(d > 0)
                def _():
                    settle_gram(cp)

            sums_narrow(2, d + 1, dn_narrow, 1, gd_v)
            sums_wide(0, d + 1, up_wide, 0, gu_v)

        return 0

    sums_narrow(2, 0, dn_narrow, 1, gd_v, True)
    sums_wide(0, 0, up_wide, 0, gu_v, True)
    pl.semaphore_wait(barrier, len(peers))
    for cp in (2, 0):
        send_sums(cp, 0)
    lax.fori_loop(0, PAIRS, pair, 0)

    wait_narrow(1)
    down_out = pltpu.make_async_copy(dn_narrow.at[PAIRS], down_img, out_sem.at[2])
    down_out.start()
    for k in range(GROUPS):
        wait_wide(0, k)
    up_out = pltpu.make_async_copy(up_wide.at[PAIRS], up_img, out_sem.at[3])
    up_out.start()
    for cp in range(4):
        last_tensor(cp)
    for w in range(2):
        last_wide(w)
        last_narrow(w)
    pltpu.make_async_copy(qn_v, up_q, out_sem.at[0]).wait()
    pltpu.make_async_copy(qw_v, down_q, out_sem.at[1]).wait()
    down_out.wait()
    up_out.wait()


def finish(scales, up_q, up_img, down_q, down_img, up_a, up_b, down_a, down_b, uq, ui, dq, di, ua, ub, da, db, sem):
    up_scale, down_scale, scale = scales
    loads = [
        pltpu.make_async_copy(src, dst, sem.at[i])
        for i, (src, dst) in enumerate(((up_q, uq), (down_q, dq), (down_img, di), (up_img, ui)))
    ]
    for load in loads:
        load.start()
    stores = [
        pltpu.make_async_copy(src, dst, sem.at[4 + i])
        for i, (src, dst) in enumerate(((ua, up_a), (da, down_a), (db, down_b), (ub, up_b)))
    ]
    loads[0].wait()
    ua[...] = uq[...].astype(jnp.float32) * up_scale
    stores[0].start()
    loads[1].wait()
    da[...] = dq[...].astype(jnp.float32) * down_scale
    stores[1].start()
    tiles = ub.shape[1] // LANES // GROUPS
    span = tiles // NY
    loads[2].wait()
    for k in range(GROUPS):
        for h in range(2):
            for yy in range(NY):
                lo = (k * NY + yy) * LANES
                piece = di[(2 * k + h) * NY + yy]
                db[HALF * h : HALF * h + HALF, lo : lo + LANES] = piece.astype(jnp.float32) * scale
    stores[2].start()
    loads[3].wait()
    for k in range(GROUPS):
        for h in range(2):
            for t in range(tiles):
                yy, n = place(t, span, k)
                lo = (k * tiles + t) * LANES
                piece = ui[(2 * k + h) * NY + yy, n]
                ub[HALF * h : HALF * h + HALF, lo : lo + LANES] = piece.astype(jnp.float32) * scale
    stores[3].start()
    for store in stores:
        store.wait()


def local(x_in, grad_up, hidden_act, grad_down, sketch_up, sketch_down):
    tokens, n_narrow = x_in.shape
    n_wide = grad_up.shape[1]
    tail = (HALF, LANES)
    piece = (n_wide // LANES // GROUPS // NY + 1,) + tail
    bf16, f32 = jnp.bfloat16, jnp.float32
    dma = pltpu.SemaphoreType.DMA
    vmem = pltpu.VMEM
    scratch = [
        vmem((tokens, n_narrow), bf16),
        vmem((tokens, n_wide), bf16),
        vmem((tokens, n_wide), bf16),
        vmem((tokens, n_narrow), bf16),
        vmem((R, n_wide), bf16),
        vmem((R, n_narrow), bf16),
        vmem((R, n_narrow), bf16),
        vmem((R, n_wide), bf16),
        vmem((PAIRS + 1, SLOTS) + piece, bf16),
        vmem((PAIRS, SLOTS) + tail, bf16),
        vmem((PAIRS, SLOTS) + piece, bf16),
        vmem((PAIRS + 1, SLOTS) + tail, bf16),
        vmem((2, PAIRS, SLOTS) + piece, bf16),
        vmem((2, PAIRS, NZ, NY - 1) + piece, bf16),
        vmem((2,) + piece, f32),
        vmem((2, PAIRS, NZ) + piece, bf16),
        vmem((2, PAIRS, NZ - 1) + piece, bf16),
        vmem((2, PAIRS, SLOTS) + tail, bf16),
        vmem((2, PAIRS, SLOTS) + tail, bf16),
        vmem((4, PAIRS, NT, R, tokens), bf16),
        vmem((GROUPS, R, R), f32),
        vmem((4, PAIRS, NT, 8, LANES), f32),
        dma((6,)), dma((4,)), dma((2,)), dma((2, NZ)), dma((2,)), dma((2,)),
        dma((2,)), dma((2, NZ - 1)), dma((2, GROUPS)),
        dma((2,)), dma((2,)), dma((2,)), dma((2,)),
        dma((4,)), dma((4, PAIRS)), dma((4,)), dma((4, PAIRS)),
        dma((2,)), dma((2, 2)), dma((2, 2)), dma((2,)),
        dma((2,)), dma((2,)), dma((2, NZ - 1)), dma((2, GROUPS)),
    ]
    panels = pl.pallas_call(
        kernel,
        out_shape=(
            jax.ShapeDtypeStruct((R, n_narrow), bf16),
            jax.ShapeDtypeStruct((SLOTS,) + piece, bf16),
            jax.ShapeDtypeStruct((R, n_wide), bf16),
            jax.ShapeDtypeStruct((SLOTS,) + tail, bf16),
        ),
        in_specs=[pl.BlockSpec(memory_space=pl.ANY)] * 6,
        out_specs=[pl.BlockSpec(memory_space=pl.ANY)] * 4,
        scratch_shapes=scratch,
        compiler_params=pltpu.CompilerParams(
            collective_id=0, has_side_effects=True, vmem_limit_bytes=56 * 2**20
        ),
    )(x_in, grad_up, hidden_act, grad_down, sketch_up, sketch_down)
    width = lax.axis_size("tensor")
    scales = (
        math.sqrt(n_narrow * width),
        math.sqrt(n_wide * width),
        1.0 / math.sqrt(tokens * lax.axis_size("dp")),
    )
    outs = (
        jax.ShapeDtypeStruct((R, n_narrow), f32),
        jax.ShapeDtypeStruct((R, n_wide), f32),
        jax.ShapeDtypeStruct((R, n_wide), f32),
        jax.ShapeDtypeStruct((R, n_narrow), f32),
    )
    return pl.pallas_call(
        functools.partial(finish, scales),
        out_shape=outs,
        in_specs=[pl.BlockSpec(memory_space=pl.ANY)] * 4,
        out_specs=[pl.BlockSpec(memory_space=pl.ANY)] * 4,
        scratch_shapes=[vmem(a.shape, a.dtype) for a in tuple(panels) + outs] + [dma((8,))],
        compiler_params=pltpu.CompilerParams(vmem_limit_bytes=56 * 2**20),
    )(*panels)


def solution(mesh):
    in_specs = (
        P("dp", "tensor"),
        P("dp", "tensor"),
        P("dp", "tensor"),
        P("dp", "tensor"),
        P(None, "tensor"),
        P(None, "tensor"),
    )
    out_specs = (P(None, "tensor"), P(None, "tensor"), P(None, "tensor"), P(None, "tensor"))
    return jax.shard_map(local, mesh=mesh, in_specs=in_specs, out_specs=out_specs, check_vma=False)
```
